512 devices in a mesh: aux: 8 (over y, core), orb: 64 (over z, x).
Axes of the slice: x: 4, y: 4, z: 16, core: 2. Of those that a mesh axis runs over, the one named last changes fastest.
Arguments:
- occupied: bfloat16 [8192, 2048], P('orb'), may hold values from -1.25 to 1.25
- integrals: bfloat16 [8, 64, 15, 128, 128], P('aux', 'orb'), may hold values from -0.1875 to 0.1875
- pair_mask: int32 [64, 15], P('orb'), may hold values from 0 to 1, as said below
Outputs:
- exchange: float32 [64, 15, 128, 128], P('orb', None, 'aux')
The draws below stay inside these ranges and needn't reach their ends.
Inputs may be any that keep to these rules, and one draw needn't show every extreme that they name: The list is symmetric: pair_mask[a, s] = pair_mask[a + s - 7, 14 - s]; every block is paired with itself (slot 7); slots whose partner lies outside the grid are 0; the number of kept pairs differs from block to block.
All inputs are finite; a program needn't handle non-finite values.
Results may differ from the reference program's by a relative error of at most 0.0011.
Values may be sent and summed in bfloat16 or wider, within the bound.
No kernel may reach another device: no remote copies, remote signals or barrier semaphores. Data moves between devices by JAX's collectives and lax.ppermute only.
A program may use at most 64 MiB of HBM per device.

```python
import jax
import jax.numpy as jnp
from jax import lax

ROWS = 128
OCC = 2048
REACH = 7
SPAN = 15
NBLK = 64
NBASIS = 8192
NAUX = 8


def draw_pair_mask(key, part):
    key = jax.random.fold_in(key, 11)
    first, second = jax.random.split(key)
    level = jax.random.randint(first, (NBLK, 1), 10, 95)
    upper = (jax.random.randint(second, (NBLK, REACH), 0, 100) < level).astype(jnp.int32)
    blocks = jnp.arange(NBLK, dtype=jnp.int32)[:, None]
    offsets = jnp.arange(1, REACH + 1, dtype=jnp.int32)[None, :]
    upper = upper * (blocks + offsets < NBLK).astype(jnp.int32)
    column_index = jnp.arange(NBLK, dtype=jnp.int32)
    lower = []
    for offset in range(REACH, 0, -1):
        moved = jnp.roll(upper[:, offset - 1], offset) * (column_index >= offset).astype(jnp.int32)
        lower.append(moved[:, None])
    middle = jnp.ones((NBLK, 1), jnp.int32)
    return jnp.concatenate(lower + [middle, upper], 1)


def block_scale(rng, extent, pieces, smallest, high):
    def one(dim, shards_of):
        steps = jax.random.uniform(jax.random.fold_in(jax.random.fold_in(rng, 6), dim), (shards_of,), jnp.float32, smallest / len(pieces), high / len(pieces))
        return jnp.repeat(jnp.exp(steps), extent[dim] // shards_of).reshape((-1,) + (1,) * (len(extent) - dim - 1))

    loudness = one(*pieces[0])
    for cut in pieces[1:]:
        loudness = loudness * one(*cut)
    return loudness


def gaussian(stream_key, shape, spread, limit, cuts=(), held_as=jnp.bfloat16):
    entries = spread * jax.random.normal(stream_key, shape, jnp.float32)
    if cuts:
        entries = entries * block_scale(stream_key, shape, cuts, -0.22, 0.18)
    return jnp.clip(entries, -limit, limit).astype(held_as)


def setup_inputs(seed: int = 0) -> dict:
    streams_of = jax.random.split(jax.random.key(seed), 4)
    return {
        "occupied": gaussian(streams_of[0], (NBASIS, OCC), (1.0 / (OCC * NAUX) ** 0.25), 1.25, ((0, 64),)),
        "integrals": gaussian(streams_of[1], (NAUX, NBLK, SPAN, ROWS, ROWS), (ROWS * (REACH + 1)) ** -0.5, 0.1875, ((0, 8), (1, 64))),
        "pair_mask": draw_pair_mask(jax.random.fold_in(streams_of[3], 71), 0),
    }


def reference(occupied, integrals, pair_mask):
    nblk = pair_mask.shape[0]
    span = pair_mask.shape[1]
    reach = (span - 1) // 2
    rows = integrals.shape[3]
    occ = occupied.shape[1]
    naux = integrals.shape[0]
    blocks = occupied.astype(jnp.float32).reshape(nblk, rows, occ)
    edge = jnp.zeros((reach, rows, occ), jnp.float32)
    padded = jnp.concatenate([edge, blocks, edge], 0)
    weights = pair_mask.astype(jnp.float32)

    def half(index):
        nearby = lax.dynamic_slice_in_dim(padded, index, span, 0)
        tiles = lax.dynamic_index_in_dim(integrals, index, 1, keepdims=False).astype(jnp.float32)
        tiles = tiles * lax.dynamic_index_in_dim(weights, index, 0, keepdims=False)[None, :, None, None]
        return jnp.einsum("pomn,onk->pmk", tiles, nearby).astype(jnp.bfloat16)

    halfway = lax.map(half, jnp.arange(nblk, dtype=jnp.int32)).astype(jnp.float32)
    edge_half = jnp.zeros((reach, naux, rows, occ), jnp.float32)
    padded_half = jnp.concatenate([edge_half, halfway, edge_half], 0)

    def gram(index):
        nearby = lax.dynamic_slice_in_dim(padded_half, index, span, 0)
        own = lax.dynamic_index_in_dim(halfway, index, 0, keepdims=False)
        tiles = jnp.einsum("pmk,opnk->omn", own, nearby)
        return tiles * lax.dynamic_index_in_dim(weights, index, 0, keepdims=False)[:, None, None]

    return lax.map(gram, jnp.arange(nblk, dtype=jnp.int32))
```

```python
import jax
import jax.numpy as jnp
from jax import lax
from jax.sharding import Mesh, PartitionSpec as P

ROWS = 128
WIDE = 256
SPAN = 15


def moved(x, axis, by):
    n = lax.axis_size(axis)
    return lax.ppermute(x, axis, [(i, (i + by) % n) for i in range(n)])


def per_device(occupied, integrals, pair_mask):
    x = lax.axis_index("x")
    core = lax.axis_index("core")
    mask_row = pair_mask[0]
    tiles = integrals[0, 0] * mask_row.astype(jnp.bfloat16)[:, None, None]

    from_left = moved(tiles, "x", 1)
    from_right = moved(tiles, "x", -1)
    from_far = moved(tiles, "x", 2)
    by_turn = [tiles, from_right, from_far, from_left]

    mine = lax.dynamic_index_in_dim(
        occupied.reshape(ROWS, 4, 2, WIDE), core, 2, keepdims=False
    )
    plane = lax.all_to_all(mine.transpose(1, 0, 2), "x", 0, 0)
    below = moved(plane, "z", 1)
    above = moved(plane, "z", -1)
    below2 = moved(plane[1:], "z", 2)
    above2 = moved(plane[:3], "z", -2)
    window = jnp.concatenate([below2, below, plane, above, above2], 0)

    halves = []
    for turn in range(4):
        both = jnp.stack([by_turn[turn], moved(by_turn[turn], "core", 1)])
        near = lax.dynamic_slice_in_dim(window, (x + turn) % 4, SPAN, 0)
        half = jnp.einsum("pomn,onk->mpk", both, near, preferred_element_type=jnp.float32)
        halves.append(half.astype(jnp.bfloat16).reshape(ROWS, 2 * WIDE))
    half = jnp.stack(halves)
    half = lax.dynamic_slice_in_dim(jnp.concatenate([half, half]), 4 - x, 4, 0)

    down = moved(half, "z", 1)
    up = moved(half, "z", -1)
    three = jnp.stack([down, half, up])
    other = moved(three, "core", 1)
    full = jnp.concatenate([three, other], -1)
    rows = lax.dynamic_index_in_dim(
        full.reshape(3, 4, 4, 2, 16, 4 * WIDE), core, 3, keepdims=False
    )
    home = jnp.einsum(
        "xyrk,pbnk->xyrpbn", rows[1], full, preferred_element_type=jnp.float32
    ).reshape(4, 4, 16, 12, ROWS)
    to_below = jnp.einsum(
        "xyrk,bnk->xyrbn", rows[0], full[2, :3], preferred_element_type=jnp.float32
    )
    to_above = jnp.einsum(
        "xyrk,bnk->xyrbn", rows[2], full[0, 1:], preferred_element_type=jnp.float32
    )
    first = jnp.arange(3)[None, :] < jnp.arange(4)[:, None]
    far = jnp.where(first[:, None, None, :, None], to_below, to_above)
    partial = jnp.concatenate([home, far], 3).astype(jnp.bfloat16)
    partial = lax.all_to_all(partial.reshape(16, 16, SPAN, ROWS), ("x", "y"), 0, 0)
    total = partial.astype(jnp.float32).sum(0).transpose(1, 0, 2)
    far = total[12:]
    line = jnp.concatenate([moved(far, "z", 1), total[:12], moved(far, "z", -1)], 0)
    out = lax.dynamic_slice_in_dim(line, x, SPAN, 0)
    return (out * mask_row.astype(jnp.float32)[:, None, None])[None]


def solution(mesh):
    split = Mesh(mesh.devices.reshape(4, 2, 16, 4), ("y", "core", "z", "x"))
    aux, orb = ("y", "core"), ("z", "x")
    return jax.shard_map(
        per_device,
        mesh=split,
        in_specs=(P(orb, None), P(aux, orb, None, None, None), P(orb, None)),
        out_specs=P(orb, None, aux, None),
        check_vma=False,
    )
```

```python
import jax
import jax.numpy as jnp
from jax import lax
from jax.experimental import pallas as pl
from jax.experimental.pallas import tpu as pltpu
from jax.sharding import Mesh, PartitionSpec as P

ROWS = 128
WIDE = 256
SPAN = 15
PLANE = 512
F32 = jnp.float32
BF16 = jnp.bfloat16


def moved(x, axis, by):
    n = lax.axis_size(axis)
    return lax.ppermute(x, axis, [(i, (i + by) % n) for i in range(n)])


def half_kernel(tiles, below2, below, plane, above, above2, half, window):
    @pl.when(pl.program_id(0) == 0)
    def _():
        at = 0
        for part in (below2, below, plane, above, above2):
            n = part.shape[0] * ROWS
            window[pl.ds(at, n), :] = part[...].reshape(n, WIDE)
            at += n

    a = pl.program_id(0)
    near = window[pl.ds(pl.multiple_of(a * ROWS, ROWS), SPAN * ROWS), :]
    for p in range(2):
        wide = jnp.concatenate([tiles[0, p, s] for s in range(SPAN)], 1)
        made = jnp.dot(wide, near, preferred_element_type=F32)
        half[:, p * WIDE : (p + 1) * WIDE] = made.astype(BF16)


def make_half(tiles, parts):
    whole = [pl.BlockSpec(p.shape, lambda a: (0, 0, 0)) for p in parts]
    return pl.pallas_call(
        half_kernel,
        grid=(4,),
        in_specs=[pl.BlockSpec((1, 2, SPAN, ROWS, ROWS), lambda a: (a, 0, 0, 0, 0))] + whole,
        out_specs=pl.BlockSpec((ROWS, 2 * WIDE), lambda a: (a, 0)),
        out_shape=jax.ShapeDtypeStruct((PLANE, 2 * WIDE), BF16),
        scratch_shapes=[pltpu.VMEM((18 * ROWS, WIDE), BF16)],
        compiler_params=pltpu.CompilerParams(vmem_limit_bytes=32 * 2**20),
        name="make_half",
    )(tiles, *parts)


def dot_t(a, b):
    return lax.dot_general(a, b, (((1,), (1,)), ((), ())), preferred_element_type=F32)


def tile_kernel(core, own, own2, up, up2, down, down2, out, mine, lower, upper):
    shift = core[0] * 16
    for k in range(16):
        at = pl.ds(pl.multiple_of(k * 32 + shift, 16), 16)
        to = pl.ds(k * 16, 16)
        for rows, first, second in ((mine, own, own2), (lower, up, up2), (upper, down, down2)):
            rows[to, :PLANE] = first[at, :]
            rows[to, PLANE:] = second[at, :]

    def put(rows, r, n, first, second, b, m, at):
        pair = dot_t(rows[r : r + n, :PLANE], first[b : b + m, :])
        pair += dot_t(rows[r : r + n, PLANE:], second[b : b + m, :])
        out[r : r + n, at : at + m] = pair.astype(BF16)

    for i, (first, second) in enumerate(((up, up2), (own, own2), (down, down2))):
        put(mine, 0, 256, first, second, 0, PLANE, i * PLANE)
    for x in range(4):
        if x > 0:
            put(lower, x * 64, 64, down, down2, 0, x * ROWS, 3 * PLANE)
        if x < 3:
            put(upper, x * 64, 64, up, up2, (x + 1) * ROWS, (3 - x) * ROWS, 3 * PLANE + x * ROWS)


def make_tiles(core, *halves):
    vmem = pl.BlockSpec(memory_space=pltpu.VMEM)
    return pl.pallas_call(
        tile_kernel,
        in_specs=[pl.BlockSpec(memory_space=pltpu.SMEM)] + [vmem] * 6,
        out_specs=vmem,
        out_shape=jax.ShapeDtypeStruct((256, SPAN * ROWS), BF16),
        scratch_shapes=[pltpu.VMEM((256, 2 * PLANE), BF16)] * 3,
        compiler_params=pltpu.CompilerParams(vmem_limit_bytes=32 * 2**20),
        name="make_tiles",
    )(core, *halves)


def per_device(occupied, integrals, pair_mask):
    x = lax.axis_index("x")
    core = lax.axis_index("core")
    mask_row = pair_mask[0]
    tiles = integrals[0, 0] * mask_row.astype(BF16)[:, None, None]
    gathered = lax.all_gather(tiles, ("x", "core")).reshape(4, 2, SPAN, ROWS, ROWS)

    rows = lax.dynamic_slice_in_dim(occupied, core * 64, 64, 0).reshape(64, 8, WIDE)
    plane = lax.all_to_all(rows.transpose(1, 0, 2), ("x", "core"), 0, 0)
    plane = plane.reshape(4, ROWS, WIDE)
    below2 = moved(plane[1:], "z", 2)
    above2 = moved(plane[:3], "z", -2)
    below = moved(plane, "z", 1)
    above = moved(plane, "z", -1)

    own = make_half(gathered, (below2, below, plane, above, above2))
    up = moved(own, "z", 1)
    down = moved(own, "z", -1)
    own2 = moved(own, "core", 1)
    up2 = moved(up, "core", 1)
    down2 = moved(down, "core", 1)
    partial = make_tiles(core[None], own, own2, up, up2, down, down2)
    partial = lax.all_to_all(partial.reshape(16, 16, SPAN * ROWS), ("x", "y"), 0, 0)
    total = partial.astype(F32).sum(0).reshape(16, SPAN, ROWS).transpose(1, 0, 2)
    far = total[12:]
    line = jnp.concatenate([moved(far, "z", 1), total[:12], moved(far, "z", -1)], 0)
    out = lax.dynamic_slice_in_dim(line, x, SPAN, 0)
    return (out * mask_row.astype(F32)[:, None, None])[None]


def solution(mesh):
    split = Mesh(mesh.devices.reshape(4, 2, 16, 4), ("y", "core", "z", "x"))
    aux, orb = ("y", "core"), ("z", "x")
    return jax.shard_map(
        per_device,
        mesh=split,
        in_specs=(P(orb, None), P(aux, orb, None, None, None), P(orb, None)),
        out_specs=P(orb, None, aux, None),
        check_vma=False,
    )
```

```python
import jax
import jax.numpy as jnp
from jax import lax
from jax.experimental import pallas as pl
from jax.experimental.pallas import tpu as pltpu
from jax.sharding import Mesh, PartitionSpec as P

ROWS = 128
HALF = 64
COLS = 512
SPAN = 15
F32 = jnp.float32
BF16 = jnp.bfloat16
VMEM = pl.BlockSpec(memory_space=pltpu.VMEM)
SMEM = pl.BlockSpec(memory_space=pltpu.SMEM)
ROOM = pltpu.CompilerParams(vmem_limit_bytes=12 * 2**20)


def moved(x, axis, by):
    n = lax.axis_size(axis)
    return lax.ppermute(x, axis, [(i, (i + by) % n) for i in range(n)])


def orbital_kernel(core, occupied, out):
    rows = occupied[pl.ds(pl.multiple_of(core[0] * HALF, HALF), HALF), :]
    for x in range(4):
        out[x] = rows[:, x * COLS : (x + 1) * COLS]


def integral_kernel(mask, integrals, out):
    for s in range(SPAN):
        tile = integrals[s]
        tile = jnp.where(mask[0, s] != 0, tile, jnp.zeros_like(tile))
        for core in range(2):
            for y in range(4):
                at = (2 * y + core) * 16
                for x in range(4):
                    out[x, core, s, y * 16 : y * 16 + 16, :] = tile[at : at + 16]


def half_kernel(core, tiles, below2, below, plane, above, above2, first, second, half, window):
    c = core[0]

    def place(part, blocks, at, where):
        for b in range(blocks.shape[0]):
            to = pl.multiple_of(at * ROWS + b * ROWS + where * HALF, HALF)
            window[pl.ds(to, HALF), :] = part[b]

    at = 0
    others = (first.at[4:7], second.at[0:4], first.at[0:4], second.at[4:8], first.at[7:10])
    for mine, other in zip((below2, below, plane, above, above2), others):
        place(mine, mine, at, c)
        place(other, mine, at, 1 - c)
        at += mine.shape[0]
    for a in range(4):
        near = window[a * ROWS : (a + SPAN) * ROWS, :]
        wide = jnp.concatenate(
            [tiles[2 * a : 2 * a + 2, s].reshape(2 * HALF, ROWS) for s in range(SPAN)], 1
        )
        made = jnp.dot(wide, near, preferred_element_type=F32).astype(BF16)
        half[a * HALF : (a + 1) * HALF, :COLS] = made[:HALF]
        half[a * HALF : (a + 1) * HALF, COLS:] = made[HALF:]


def dot_t(a, b):
    return lax.dot_general(a, b, (((1,), (1,)), ((), ())), preferred_element_type=F32)


def tile_kernel(core, up, own, down, up2, own2, down2, out, wide):
    c = core[0]
    for i, (mine, other) in enumerate(((up, up2), (own, own2), (down, down2))):
        for k in range(16):
            to = i * 512 + k * 32
            wide[pl.ds(pl.multiple_of(to + c * 16, 16), 16), :] = mine[k * 16 : k * 16 + 16, :]
            wide[pl.ds(pl.multiple_of(to + 16 - c * 16, 16), 16), :] = other[k * 16 : k * 16 + 16, :]
    for i in range(3):
        out[:, i * 512 : (i + 1) * 512] = dot_t(own[...], wide[i * 512 : (i + 1) * 512, :]).astype(BF16)
    for x in range(4):
        rows = slice(x * HALF, (x + 1) * HALF)
        cut = 1536 + x * ROWS
        if x > 0:
            out[rows, 1536:cut] = dot_t(up[rows, :], wide[1024 : 1024 + x * ROWS, :]).astype(BF16)
        if x < 3:
            out[rows, cut:] = dot_t(down[rows, :], wide[(x + 1) * ROWS : 512, :]).astype(BF16)


def per_device(occupied, integrals, pair_mask):
    x = lax.axis_index("x")
    core = lax.axis_index("core")[None]

    pieces = pl.pallas_call(
        orbital_kernel,
        in_specs=[SMEM, VMEM],
        out_specs=VMEM,
        out_shape=jax.ShapeDtypeStruct((4, HALF, COLS), BF16),
        compiler_params=ROOM,
        name="cut_orbitals",
    )(core, occupied)
    plane = lax.all_to_all(pieces, "x", 0, 0)

    tiles = pl.pallas_call(
        integral_kernel,
        in_specs=[SMEM, VMEM],
        out_specs=VMEM,
        out_shape=jax.ShapeDtypeStruct((4, 2, SPAN, HALF, ROWS), BF16),
        compiler_params=ROOM,
        name="cut_integrals",
    )(pair_mask, integrals[0, 0])
    tiles = lax.all_to_all(tiles.reshape(8, SPAN, HALF, ROWS), ("x", "core"), 0, 0)

    below2 = moved(plane[1:], "z", 2)
    above2 = moved(plane[:3], "z", -2)
    below = moved(plane, "z", 1)
    above = moved(plane, "z", -1)
    first = moved(jnp.concatenate([plane, below2, above2]), "core", 1)
    second = moved(jnp.concatenate([below, above]), "core", 1)

    own = pl.pallas_call(
        half_kernel,
        in_specs=[SMEM] + [VMEM] * 8,
        out_specs=VMEM,
        out_shape=jax.ShapeDtypeStruct((4 * HALF, 2 * COLS), BF16),
        scratch_shapes=[pltpu.VMEM((18 * ROWS, COLS), BF16)],
        compiler_params=ROOM,
        name="make_half",
    )(core, tiles, below2, below, plane, above, above2, first, second)

    up = moved(own, "z", 1)
    down = moved(own, "z", -1)
    own2 = moved(own, "core", 1)
    up2 = moved(up, "core", 1)
    down2 = moved(down, "core", 1)
    partial = pl.pallas_call(
        tile_kernel,
        in_specs=[SMEM] + [VMEM] * 6,
        out_specs=VMEM,
        out_shape=jax.ShapeDtypeStruct((256, SPAN * ROWS), BF16),
        scratch_shapes=[pltpu.VMEM((12 * ROWS, 2 * COLS), BF16)],
        compiler_params=ROOM,
        name="make_tiles",
    )(core, up, own, down, up2, own2, down2)
    partial = lax.all_to_all(partial.reshape(16, 16, SPAN * ROWS), ("x", "y"), 0, 0)
    total = partial.astype(F32).sum(0).reshape(16, SPAN, ROWS).transpose(1, 0, 2)
    far = total[12:]
    line = jnp.concatenate([moved(far, "z", 1), total[:12], moved(far, "z", -1)], 0)
    out = lax.dynamic_slice_in_dim(line, x, SPAN, 0)
    return (out * pair_mask[0].astype(F32)[:, None, None])[None]


def solution(mesh):
    split = Mesh(mesh.devices.reshape(4, 2, 16, 4), ("y", "core", "z", "x"))
    aux, orb = ("y", "core"), ("z", "x")
    return jax.shard_map(
        per_device,
        mesh=split,
        in_specs=(P(orb, None), P(aux, orb, None, None, None), P(orb, None)),
        out_specs=P(orb, None, aux, None),
        check_vma=False,
    )
```

```python
import jax
import jax.numpy as jnp
from jax import lax
from jax.experimental import pallas as pl
from jax.experimental.pallas import tpu as pltpu
from jax.sharding import Mesh, PartitionSpec as P

ROWS = 128
HALF = 64
COLS = 512
SPAN = 15
F32 = jnp.float32
BF16 = jnp.bfloat16
VMEM = pl.BlockSpec(memory_space=pltpu.VMEM)
SMEM = pl.BlockSpec(memory_space=pltpu.SMEM)


def call(kernel, name, specs, shape, dtype, *args, scratch=()):
    return pl.pallas_call(
        kernel,
        in_specs=specs,
        out_specs=VMEM,
        out_shape=jax.ShapeDtypeStruct(shape, dtype),
        scratch_shapes=scratch,
        compiler_params=pltpu.CompilerParams(vmem_limit_bytes=12 * 2**20),
        name=name,
    )(*args)


def swapped(x):
    return lax.ppermute(x, "core", [(0, 1), (1, 0)])


def moved(x, by):
    n = lax.axis_size("z")
    return lax.ppermute(x, "z", [(i, (i + by) % n) for i in range(n)])


def sided(x, by):
    n = lax.axis_size("z")
    pairs = [(i, (i + by) % n) for i in range(n)]
    pairs += [(n + i, n + (i - by) % n) for i in range(n)]
    return lax.ppermute(x, ("core", "z"), pairs)


def orbital_kernel(occupied, out):
    for x in range(4):
        out[x] = occupied[:, x * COLS : (x + 1) * COLS]


def integral_kernel(mask, integrals, out):
    for s in range(SPAN):
        tile = integrals[s]
        tile = jnp.where(mask[0, s] != 0, tile, jnp.zeros_like(tile))
        for x in range(4):
            out[x, 0, s] = tile[:HALF]
            out[x, 1, s] = tile[HALF:]


def half_kernel(core, tiles, plane, mine, other, half, window):
    c = core[0]

    def place(part, first, n, at):
        window[pl.ds(pl.multiple_of(at * ROWS, ROWS), n * ROWS), :] = part[
            first : first + n
        ].reshape(n * ROWS, COLS)

    place(plane, 0, 4, 7)
    place(mine, 0, 3, c * 15)
    place(mine, 3, 4, 3 + c * 8)
    place(other, 0, 3, 15 - c * 15)
    place(other, 3, 4, 11 - c * 8)
    for a in range(4):
        near = window[a * ROWS : (a + SPAN) * ROWS, :]
        wide = jnp.concatenate(
            [tiles[2 * a : 2 * a + 2, s].reshape(2 * HALF, ROWS) for s in range(SPAN)], 1
        )
        made = jnp.dot(wide, near, preferred_element_type=F32).astype(BF16)
        half[a * HALF : (a + 1) * HALF, :COLS] = made[:HALF]
        half[a * HALF : (a + 1) * HALF, COLS:] = made[HALF:]


def dot_t(a, b):
    return lax.dot_general(a, b, (((1,), (1,)), ((), ())), preferred_element_type=F32)


def interleave(core, mine, other, wide, at):
    for b in range(4):
        to = at + b * ROWS
        rows = slice(b * HALF, (b + 1) * HALF)
        wide[pl.ds(pl.multiple_of(to + core * HALF, HALF), HALF), :] = mine[rows, :]
        wide[pl.ds(pl.multiple_of(to + HALF - core * HALF, HALF), HALF), :] = other[rows, :]


def home_kernel(core, own, own2, side, side2, out, wide):
    c = core[0]
    interleave(c, side, side2, wide, 0)
    interleave(c, own, own2, wide, 512)
    inner = wide[pl.ds(pl.multiple_of(512 + c * 256, 256), 256), :]
    for k, rows in ((c, own), (1 - c, own2)):
        left = rows[...]
        outer = dot_t(left, wide[0:512, :]).astype(BF16)
        within = dot_t(left, inner).astype(BF16)
        for x in range(4):
            for j in range(4):
                at = slice(x * HALF + j * 16, x * HALF + j * 16 + 16)
                out[x * 8 + k * 4 + j, :, :512] = outer[at]
                out[x * 8 + k * 4 + j, :, 512:] = within[at]


def far_kernel(core, side, side2, other, other2, out, low, high, below, above):
    c = core[0]

    @pl.when(c == 0)
    def _():
        interleave(0, side, side2, low, 0)
        interleave(0, other2, other, high, 0)

    @pl.when(c == 1)
    def _():
        interleave(0, other, other2, low, 0)
        interleave(0, side2, side, high, 0)

    for k in range(16):
        at = pl.ds(pl.multiple_of(k * 32 + c * 16, 16), 16)
        below[k * 16 : k * 16 + 16, :] = low[at, :]
        above[k * 16 : k * 16 + 16, :] = high[at, :]
    for x in range(4):
        rows = slice(x * HALF, (x + 1) * HALF)
        cut = x * ROWS
        made = []
        if x > 0:
            made.append(dot_t(below[rows, :], high[0:cut, :]).astype(BF16))
        if x < 3:
            made.append(dot_t(above[rows, :], low[cut + ROWS : 512, :]).astype(BF16))
        out[rows, :] = jnp.concatenate(made, 1)


def last_kernel(place, mask, home, low, high, out, line):
    for e in range(3):
        line[e] = low[:, e * ROWS : (e + 1) * ROWS]
        line[15 + e] = high[:, e * ROWS : (e + 1) * ROWS]
    for b in range(4):
        line[3 + b] = home[0, :, b * ROWS : (b + 1) * ROWS]
        line[11 + b] = home[1, :, b * ROWS : (b + 1) * ROWS]
        at = 512 + (b % 2) * ROWS
        line[7 + b] = home[b // 2, :, at : at + ROWS]
    x = place[0]
    for s in range(SPAN):
        out[s] = line[x + s] * mask[0, s].astype(F32)


def per_device(occupied, integrals, pair_mask):
    x = lax.axis_index("x")[None]
    c = lax.axis_index("core")
    core = c[None]

    pieces = call(orbital_kernel, "cut_orbitals", [VMEM], (4, ROWS, COLS), BF16, occupied)
    plane = lax.all_to_all(pieces, "x", 0, 0)

    tiles = call(
        integral_kernel, "cut_integrals", [SMEM, VMEM], (4, 2, SPAN, HALF, ROWS), BF16,
        pair_mask, integrals[0, 0],
    )
    tiles = lax.all_to_all(tiles.reshape(8, SPAN, HALF, ROWS), ("x", "core"), 0, 0)

    near2 = sided(lax.dynamic_slice_in_dim(plane, 1 - c, 3, 0), 2)
    near = sided(plane, 1)
    mine = jnp.concatenate([near2, near])
    other = swapped(mine)

    own = call(
        half_kernel, "make_half", [SMEM] + [VMEM] * 4, (4 * HALF, 2 * COLS), BF16,
        core, tiles, plane, mine, other,
        scratch=[pltpu.VMEM((18 * ROWS, COLS), BF16)],
    )

    side = sided(own, 1)
    own2 = swapped(own)
    side2 = sided(own2, 1)
    home = call(
        home_kernel, "make_home", [SMEM] + [VMEM] * 4, (32, 16, 768), BF16,
        core, own, own2, side, side2,
        scratch=[pltpu.VMEM((1024, 2 * COLS), BF16)],
    )
    home = lax.all_to_all(home, ("x", "y", "core"), 0, 0)
    home = home.reshape(16, 2, 16, 768).astype(F32).sum(0)

    far = call(
        far_kernel, "make_far", [SMEM] + [VMEM] * 4, (256, 384), BF16,
        core, side, side2, swapped(side), swapped(side2),
        scratch=[pltpu.VMEM((512, 2 * COLS), BF16)] * 2 + [pltpu.VMEM((256, 2 * COLS), BF16)] * 2,
    )
    far = lax.all_to_all(far.reshape(16, 16, 384), ("x", "y"), 0, 0)
    far = far.astype(F32).sum(0)
    out = call(
        last_kernel, "join", [SMEM, SMEM] + [VMEM] * 3, (SPAN, 16, ROWS), F32,
        x, pair_mask, home, moved(far, 1), moved(far, -1),
        scratch=[pltpu.VMEM((18, 16, ROWS), F32)],
    )
    return out[None]


def solution(mesh):
    split = Mesh(mesh.devices.reshape(4, 2, 16, 4), ("y", "core", "z", "x"))
    aux, orb = ("y", "core"), ("z", "x")
    return jax.shard_map(
        per_device,
        mesh=split,
        in_specs=(P(orb, None), P(aux, orb, None, None, None), P(orb, None)),
        out_specs=P(orb, None, aux, None),
        check_vma=False,
    )
```

```python
import jax
import jax.numpy as jnp
from jax import lax
from jax.experimental import pallas as pl
from jax.experimental.pallas import tpu as pltpu
from jax.sharding import Mesh, PartitionSpec as P

ROWS = 128
HALF = 64
COLS = 512
SPAN = 15
F32 = jnp.float32
BF16 = jnp.bfloat16
VMEM = pl.BlockSpec(memory_space=pltpu.VMEM)
SMEM = pl.BlockSpec(memory_space=pltpu.SMEM)
ANY = pl.BlockSpec(memory_space=pl.ANY)


def call(kernel, name, specs, shape, dtype, *args, scratch=(), out=VMEM):
    return pl.pallas_call(
        kernel,
        in_specs=specs,
        out_specs=out,
        out_shape=jax.ShapeDtypeStruct(shape, dtype),
        scratch_shapes=scratch,
        compiler_params=pltpu.CompilerParams(vmem_limit_bytes=12 * 2**20),
        name=name,
    )(*args)


def moved(x, axis, by):
    n = lax.axis_size(axis)
    return lax.ppermute(x, axis, [(i, (i + by) % n) for i in range(n)])


def swapped(x):
    return moved(x, "core", 1)


def sided(x, by):
    n = lax.axis_size("z")
    pairs = [(i, (i + by) % n) for i in range(n)]
    pairs += [(n + i, n + (i - by) % n) for i in range(n)]
    return lax.ppermute(x, ("core", "z"), pairs)


def orbital_kernel(occupied, out, sems):
    copies = [
        pltpu.make_async_copy(occupied.at[:, pl.ds(x * COLS, COLS)], out.at[x], sems.at[x])
        for x in range(4)
    ]
    for copy in copies:
        copy.start()
    for copy in copies:
        copy.wait()


def integral_kernel(mask, integrals, out):
    for s in range(SPAN):
        tile = integrals[s]
        tile = jnp.where(mask[0, s] != 0, tile, jnp.zeros_like(tile))
        for core in range(2):
            for k in range(4):
                at = k * 32 + core * 16
                for x in range(4):
                    out[x, core, s, k * 16 : k * 16 + 16, :] = tile[at : at + 16]


def half_kernel(core, tiles, plane, mine, other, half, window, sems):
    c = core[0]
    moves = (
        (plane, 0, 4, 7),
        (mine, 0, 3, c * 15),
        (mine, 3, 4, 3 + c * 8),
        (other, 0, 3, 15 - c * 15),
        (other, 3, 4, 11 - c * 8),
    )
    copies = [
        pltpu.make_async_copy(part.at[pl.ds(first, n)], window.at[pl.ds(at, n)], sems.at[i])
        for i, (part, first, n, at) in enumerate(moves)
    ]
    for copy in copies:
        copy.start()
    for copy in copies:
        copy.wait()
    for a in range(4):
        near = window[a : a + SPAN].reshape(SPAN * ROWS, COLS)
        wide = jnp.concatenate(
            [tiles[2 * a : 2 * a + 2, s].reshape(2 * HALF, ROWS) for s in range(SPAN)], 1
        )
        made = jnp.dot(wide, near, preferred_element_type=F32).astype(BF16)
        half[a * HALF : (a + 1) * HALF, :COLS] = made[:HALF]
        half[a * HALF : (a + 1) * HALF, COLS:] = made[HALF:]


def dot_t(a, b):
    return lax.dot_general(a, b, (((1,), (1,)), ((), ())), preferred_element_type=F32)


def interleave(c, mine, other, wide, at):
    for k in range(16):
        to = at + k * 32
        rows = slice(k * 16, k * 16 + 16)
        wide[pl.ds(pl.multiple_of(to + c * 16, 16), 16), :] = mine[rows, :]
        wide[pl.ds(pl.multiple_of(to + 16 - c * 16, 16), 16), :] = other[rows, :]


def inner_kernel(core, own, own2, out, wide):
    interleave(core[0], own, own2, wide, 0)
    out[...] = dot_t(own[...], wide[...]).astype(BF16)


def tile_kernel(core, inner, own, up, down, up2, down2, out, wide):
    interleave(core[0], up, up2, wide, 0)
    interleave(core[0], down, down2, wide, 512)
    out[:, 0:512] = dot_t(own[...], wide[0:512, :]).astype(BF16)
    out[:, 512:1024] = inner[...]
    out[:, 1024:1536] = dot_t(own[...], wide[512:1024, :]).astype(BF16)
    for x in range(4):
        rows = slice(x * HALF, (x + 1) * HALF)
        cut = 1536 + x * ROWS
        if x > 0:
            out[rows, 1536:cut] = dot_t(up[rows, :], wide[512 : 512 + x * ROWS, :]).astype(BF16)
        if x < 3:
            out[rows, cut:] = dot_t(down[rows, :], wide[(x + 1) * ROWS : 512, :]).astype(BF16)


def sum_kernel(parts, out):
    for t in range(SPAN):
        total = parts[0, :, t * ROWS : (t + 1) * ROWS].astype(F32)
        for k in range(1, 16):
            total += parts[k, :, t * ROWS : (t + 1) * ROWS].astype(F32)
        out[t] = total


def per_device(occupied, integrals, pair_mask):
    x = lax.axis_index("x")
    c = lax.axis_index("core")
    core = c[None]

    pieces = call(
        orbital_kernel, "cut_orbitals", [ANY], (4, ROWS, COLS), BF16, occupied,
        scratch=[pltpu.SemaphoreType.DMA((4,))], out=ANY,
    )
    plane = lax.all_to_all(pieces, "x", 0, 0)

    tiles = call(
        integral_kernel, "cut_integrals", [SMEM, VMEM], (4, 2, SPAN, HALF, ROWS), BF16,
        pair_mask, integrals[0, 0],
    )
    tiles = lax.all_to_all(tiles.reshape(8, SPAN, HALF, ROWS), ("x", "core"), 0, 0)

    two_away = sided(lax.dynamic_slice_in_dim(plane, 1 - c, 3, 0), 2)
    one_away = sided(plane, 1)
    mine = jnp.concatenate([two_away, one_away])
    other = swapped(mine)

    own = call(
        half_kernel, "make_half", [SMEM, VMEM] + [ANY] * 3, (4 * HALF, 2 * COLS), BF16,
        core, tiles, plane, mine, other,
        scratch=[pltpu.VMEM((18, ROWS, COLS), BF16), pltpu.SemaphoreType.DMA((5,))],
    )

    up = moved(own, "z", 1)
    down = moved(own, "z", -1)
    own2 = swapped(own)
    inner = call(
        inner_kernel, "make_inner", [SMEM] + [VMEM] * 2, (256, 512), BF16, core, own, own2,
        scratch=[pltpu.VMEM((512, 2 * COLS), BF16)],
    )
    inner, up, down = lax.optimization_barrier((inner, up, down))
    partial = call(
        tile_kernel, "make_tiles", [SMEM] + [VMEM] * 6, (256, SPAN * ROWS), BF16,
        core, inner, own, up, down, swapped(up), swapped(down),
        scratch=[pltpu.VMEM((1024, 2 * COLS), BF16)],
    )
    partial = lax.all_to_all(partial.reshape(16, 16, SPAN * ROWS), ("x", "y"), 0, 0)
    total = call(sum_kernel, "sum_parts", [VMEM], (SPAN, 16, ROWS), F32, partial)
    far = total[12:]
    line = jnp.concatenate([moved(far, "z", 1), total[:12], moved(far, "z", -1)], 0)
    out = lax.dynamic_slice_in_dim(line, x, SPAN, 0)
    return (out * pair_mask[0].astype(F32)[:, None, None])[None]


def solution(mesh):
    split = Mesh(mesh.devices.reshape(4, 2, 16, 4), ("y", "core", "z", "x"))
    aux, orb = ("y", "core"), ("z", "x")
    return jax.shard_map(
        per_device,
        mesh=split,
        in_specs=(P(orb, None), P(aux, orb, None, None, None), P(orb, None)),
        out_specs=P(orb, None, aux, None),
        check_vma=False,
    )
```

```python
import jax
import jax.numpy as jnp
from jax import lax
from jax.experimental import pallas as pl
from jax.experimental.pallas import tpu as pltpu
from jax.sharding import Mesh, PartitionSpec as P

ROWS = 128
HALF = 64
COLS = 512
SPAN = 15
F32 = jnp.float32
BF16 = jnp.bfloat16
VMEM = pl.BlockSpec(memory_space=pltpu.VMEM)
SMEM = pl.BlockSpec(memory_space=pltpu.SMEM)
HBM = pl.BlockSpec(memory_space=pltpu.HBM)
ANY = pl.BlockSpec(memory_space=pl.ANY)


def call(kernel, name, specs, shape, dtype, *args, scratch=(), out=VMEM):
    return pl.pallas_call(
        kernel,
        in_specs=specs,
        out_specs=out,
        out_shape=jax.ShapeDtypeStruct(shape, dtype),
        scratch_shapes=scratch,
        compiler_params=pltpu.CompilerParams(vmem_limit_bytes=12 * 2**20),
        name=name,
    )(*args)


def moved(x, axis, by):
    n = lax.axis_size(axis)
    return lax.ppermute(x, axis, [(i, (i + by) % n) for i in range(n)])


def swapped(x):
    return moved(x, "core", 1)


def orbital_kernel(core, occupied, out, sems):
    rows = pl.ds(pl.multiple_of(core[0] * HALF, HALF), HALF)
    copies = [
        pltpu.make_async_copy(occupied.at[rows, pl.ds(x * COLS, COLS)], out.at[x], sems.at[x])
        for x in range(4)
    ]
    for copy in copies:
        copy.start()
    for copy in copies:
        copy.wait()


def integral_kernel(mask, integrals, out):
    for s in range(SPAN):
        tile = integrals[s]
        tile = jnp.where(mask[0, s] != 0, tile, jnp.zeros_like(tile))
        for core in range(2):
            for k in range(4):
                at = k * 32 + core * 16
                for x in range(4):
                    out[x, core, s, k * 16 : k * 16 + 16, :] = tile[at : at + 16]


def half_kernel(core, tiles, below2, below, plane, above, above2, first, second, half, window, sems):
    c = core[0]
    moves = ((first, 4, 3, 0), (second, 0, 4, 3), (first, 0, 4, 7), (second, 4, 4, 11), (first, 7, 3, 15))
    copies = [
        pltpu.make_async_copy(part.at[pl.ds(at, n)], window.at[pl.ds(to, n), 1 - c], sems.at[i])
        for i, (part, at, n, to) in enumerate(moves)
    ]
    for copy in copies:
        copy.start()
    at = 0
    for part in (below2, below, plane, above, above2):
        for b in range(part.shape[0]):
            window[at, c] = part[b]
            at += 1
    for copy in copies:
        copy.wait()
    for a in range(4):
        near = window[a : a + SPAN].reshape(SPAN * ROWS, COLS)
        wide = jnp.concatenate(
            [tiles[2 * a : 2 * a + 2, s].reshape(2 * HALF, ROWS) for s in range(SPAN)], 1
        )
        made = jnp.dot(wide, near, preferred_element_type=F32).astype(BF16)
        half[a * HALF : (a + 1) * HALF, :COLS] = made[:HALF]
        half[a * HALF : (a + 1) * HALF, COLS:] = made[HALF:]


def dot_t(a, b):
    return lax.dot_general(a, b, (((1,), (1,)), ((), ())), preferred_element_type=F32)


def interleave(c, mine, other, wide, at):
    for k in range(16):
        to = at + k * 32
        rows = slice(k * 16, k * 16 + 16)
        wide[pl.ds(pl.multiple_of(to + c * 16, 16), 16), :] = mine[rows, :]
        wide[pl.ds(pl.multiple_of(to + 16 - c * 16, 16), 16), :] = other[rows, :]


def tile_kernel(core, up, own, down, up2, own2, down2, out, wide):
    for i, (mine, other) in enumerate(((up, up2), (own, own2), (down, down2))):
        interleave(core[0], mine, other, wide, i * 512)
    for i in range(3):
        out[:, i * 512 : (i + 1) * 512] = dot_t(own[...], wide[i * 512 : (i + 1) * 512, :]).astype(BF16)
    for x in range(4):
        rows = slice(x * HALF, (x + 1) * HALF)
        cut = 1536 + x * ROWS
        if x > 0:
            out[rows, 1536:cut] = dot_t(up[rows, :], wide[1024 : 1024 + x * ROWS, :]).astype(BF16)
        if x < 3:
            out[rows, cut:] = dot_t(down[rows, :], wide[(x + 1) * ROWS : 512, :]).astype(BF16)


def sum_kernel(parts, out):
    for t in range(SPAN):
        total = parts[0, :, t * ROWS : (t + 1) * ROWS].astype(F32)
        for k in range(1, 16):
            total += parts[k, :, t * ROWS : (t + 1) * ROWS].astype(F32)
        out[t] = total


def per_device(occupied, integrals, pair_mask):
    x = lax.axis_index("x")
    c = lax.axis_index("core")
    core = c[None]

    pieces = call(
        orbital_kernel, "cut_orbitals", [SMEM, HBM], (4, HALF, COLS), BF16, core, occupied,
        scratch=[pltpu.SemaphoreType.DMA((4,))], out=HBM,
    )
    plane = lax.all_to_all(pieces, "x", 0, 0)

    tiles = call(
        integral_kernel, "cut_integrals", [SMEM, VMEM], (4, 2, SPAN, HALF, ROWS), BF16,
        pair_mask, integrals[0, 0],
    )
    tiles = lax.all_to_all(tiles.reshape(8, SPAN, HALF, ROWS), ("x", "core"), 0, 0)

    below2 = moved(plane[1:], "z", 2)
    above2 = moved(plane[:3], "z", -2)
    below = moved(plane, "z", 1)
    above = moved(plane, "z", -1)
    first = swapped(jnp.concatenate([plane, below2, above2]))
    tiles, above = lax.optimization_barrier((tiles, above))
    second = swapped(jnp.concatenate([below, above]))

    own = call(
        half_kernel, "make_half", [SMEM] + [VMEM] * 6 + [ANY] * 2, (4 * HALF, 2 * COLS), BF16,
        core, tiles, below2, below, plane, above, above2, first, second,
        scratch=[pltpu.VMEM((18, 2, HALF, COLS), BF16), pltpu.SemaphoreType.DMA((5,))],
    )

    up = moved(own, "z", 1)
    down = moved(own, "z", -1)
    own2 = swapped(own)
    partial = call(
        tile_kernel, "make_tiles", [SMEM] + [VMEM] * 6, (256, SPAN * ROWS), BF16,
        core, up, own, down, swapped(up), own2, swapped(down),
        scratch=[pltpu.VMEM((1536, 2 * COLS), BF16)],
    )
    partial = lax.all_to_all(partial.reshape(16, 16, SPAN * ROWS), ("x", "y"), 0, 0)
    total = call(sum_kernel, "sum_parts", [VMEM], (SPAN, 16, ROWS), F32, partial)
    far = total[12:]
    line = jnp.concatenate([moved(far, "z", 1), total[:12], moved(far, "z", -1)], 0)
    out = lax.dynamic_slice_in_dim(line, x, SPAN, 0)
    return (out * pair_mask[0].astype(F32)[:, None, None])[None]


def solution(mesh):
    split = Mesh(mesh.devices.reshape(4, 2, 16, 4), ("y", "core", "z", "x"))
    aux, orb = ("y", "core"), ("z", "x")
    return jax.shard_map(
        per_device,
        mesh=split,
        in_specs=(P(orb, None), P(aux, orb, None, None, None), P(orb, None)),
        out_specs=P(orb, None, aux, None),
        check_vma=False,
    )
```

```python
import jax
import jax.numpy as jnp
from jax import lax
from jax.experimental import pallas as pl
from jax.experimental.pallas import tpu as pltpu
from jax.sharding import Mesh, PartitionSpec as P

ROWS = 128
HALF = 64
COLS = 512
SPAN = 15
F32 = jnp.float32
BF16 = jnp.bfloat16
VMEM = pl.BlockSpec(memory_space=pltpu.VMEM)
SMEM = pl.BlockSpec(memory_space=pltpu.SMEM)
HBM = pl.BlockSpec(memory_space=pltpu.HBM)
ANY = pl.BlockSpec(memory_space=pl.ANY)


def call(kernel, name, specs, shape, dtype, *args, scratch=(), out=VMEM):
    return pl.pallas_call(
        kernel,
        in_specs=specs,
        out_specs=out,
        out_shape=jax.ShapeDtypeStruct(shape, dtype),
        scratch_shapes=scratch,
        compiler_params=pltpu.CompilerParams(vmem_limit_bytes=12 * 2**20),
        name=name,
    )(*args)


def moved(x, by):
    n = lax.axis_size("z")
    return lax.ppermute(x, "z", [(i, i + by) for i in range(n) if 0 <= i + by < n])


def swapped(x):
    return lax.ppermute(x, "core", [(0, 1), (1, 0)])


def orbital_kernel(core, occupied, out, sems):
    rows = pl.ds(pl.multiple_of(core[0] * HALF, HALF), HALF)
    copies = [
        pltpu.make_async_copy(occupied.at[rows, pl.ds(x * COLS, COLS)], out.at[x], sems.at[x])
        for x in range(4)
    ]
    for copy in copies:
        copy.start()
    for copy in copies:
        copy.wait()


def integral_kernel(mask, integrals, out):
    for s in range(SPAN):
        tile = integrals[s]
        tile = jnp.where(mask[0, s] != 0, tile, jnp.zeros_like(tile))
        for core in range(2):
            for k in range(4):
                at = k * 32 + core * 16
                for x in range(4):
                    out[x, core, s, k * 16 : k * 16 + 16, :] = tile[at : at + 16]


def half_kernel(core, tiles, below2, below, plane, above, above2, first, second, half, window, sems):
    c = core[0]
    moves = ((first, 4, 3, 0), (second, 0, 4, 3), (first, 0, 4, 7), (second, 4, 4, 11), (first, 7, 3, 15))
    copies = [
        pltpu.make_async_copy(part.at[pl.ds(at, n)], window.at[pl.ds(to, n), 1 - c], sems.at[i])
        for i, (part, at, n, to) in enumerate(moves)
    ]
    for copy in copies:
        copy.start()
    at = 0
    for part in (below2, below, plane, above, above2):
        for b in range(part.shape[0]):
            window[at, c] = part[b]
            at += 1
    for copy in copies:
        copy.wait()
    for a in range(4):
        near = window[a : a + SPAN].reshape(SPAN * ROWS, COLS)
        wide = jnp.concatenate(
            [tiles[2 * a : 2 * a + 2, s].reshape(2 * HALF, ROWS) for s in range(SPAN)], 1
        )
        made = jnp.dot(wide, near, preferred_element_type=F32).astype(BF16)
        half[a * HALF : (a + 1) * HALF, :COLS] = made[:HALF]
        half[a * HALF : (a + 1) * HALF, COLS:] = made[HALF:]


def dot_t(a, b):
    return lax.dot_general(a, b, (((1,), (1,)), ((), ())), preferred_element_type=F32)


def interleave(c, mine, other, wide, at):
    for k in range(16):
        to = at + k * 32
        rows = slice(k * 16, k * 16 + 16)
        wide[pl.ds(pl.multiple_of(to + c * 16, 16), 16), :] = mine[rows, :]
        wide[pl.ds(pl.multiple_of(to + 16 - c * 16, 16), 16), :] = other[rows, :]


def tile_kernel(core, up, own, down, up2, own2, down2, out, wide):
    for i, (mine, other) in enumerate(((up, up2), (own, own2), (down, down2))):
        interleave(core[0], mine, other, wide, i * 512)
    for i in range(3):
        out[:, i * 512 : (i + 1) * 512] = dot_t(own[...], wide[i * 512 : (i + 1) * 512, :]).astype(BF16)
    for x in range(4):
        rows = slice(x * HALF, (x + 1) * HALF)
        cut = 1536 + x * ROWS
        if x > 0:
            out[rows, 1536:cut] = dot_t(up[rows, :], wide[1024 : 1024 + x * ROWS, :]).astype(BF16)
        if x < 3:
            out[rows, cut:] = dot_t(down[rows, :], wide[(x + 1) * ROWS : 512, :]).astype(BF16)


def sum_kernel(parts, out):
    for t in range(SPAN):
        total = parts[0, :, t * ROWS : (t + 1) * ROWS].astype(F32)
        for k in range(1, 16):
            total += parts[k, :, t * ROWS : (t + 1) * ROWS].astype(F32)
        out[t] = total


def per_device(occupied, integrals, pair_mask):
    x = lax.axis_index("x")
    c = lax.axis_index("core")
    core = c[None]

    pieces = call(
        orbital_kernel, "cut_orbitals", [SMEM, HBM], (4, HALF, COLS), BF16, core, occupied,
        scratch=[pltpu.SemaphoreType.DMA((4,))], out=HBM,
    )
    plane = lax.all_to_all(pieces, "x", 0, 0)

    tiles = call(
        integral_kernel, "cut_integrals", [SMEM, VMEM], (4, 2, SPAN, HALF, ROWS), BF16,
        pair_mask, integrals[0, 0],
    )
    tiles = lax.all_to_all(tiles.reshape(8, SPAN, HALF, ROWS), ("x", "core"), 0, 0)

    below2 = moved(plane[1:], 2)
    above2 = moved(plane[:3], -2)
    below = moved(plane, 1)
    above = moved(plane, -1)
    first = swapped(jnp.concatenate([plane, below2, above2]))
    tiles, above = lax.optimization_barrier((tiles, above))
    second = swapped(jnp.concatenate([below, above]))

    own = call(
        half_kernel, "make_half", [SMEM] + [VMEM] * 6 + [ANY] * 2, (4 * HALF, 2 * COLS), BF16,
        core, tiles, below2, below, plane, above, above2, first, second,
        scratch=[pltpu.VMEM((18, 2, HALF, COLS), BF16), pltpu.SemaphoreType.DMA((5,))],
    )

    up = moved(own, 1)
    down = moved(own, -1)
    own2 = swapped(own)
    partial = call(
        tile_kernel, "make_tiles", [SMEM] + [VMEM] * 6, (256, SPAN * ROWS), BF16,
        core, up, own, down, swapped(up), own2, swapped(down),
        scratch=[pltpu.VMEM((1536, 2 * COLS), BF16)],
    )
    partial = lax.all_to_all(partial.reshape(16, 16, SPAN * ROWS), ("x", "y"), 0, 0)
    total = call(sum_kernel, "sum_parts", [VMEM], (SPAN, 16, ROWS), F32, partial)
    far = total[12:]
    line = jnp.concatenate([moved(far, 1), total[:12], moved(far, -1)], 0)
    out = lax.dynamic_slice_in_dim(line, x, SPAN, 0)
    return (out * pair_mask[0].astype(F32)[:, None, None])[None]


def solution(mesh):
    split = Mesh(mesh.devices.reshape(4, 2, 16, 4), ("y", "core", "z", "x"))
    aux, orb = ("y", "core"), ("z", "x")
    return jax.shard_map(
        per_device,
        mesh=split,
        in_specs=(P(orb, None), P(aux, orb, None, None, None), P(orb, None)),
        out_specs=P(orb, None, aux, None),
        check_vma=False,
    )
```

```python
import jax
import jax.numpy as jnp
from jax import lax
from jax.experimental import pallas as pl
from jax.experimental.pallas import tpu as pltpu
from jax.sharding import Mesh, PartitionSpec as P

ROWS = 128
HALF = 64
COLS = 512
SPAN = 15
F32 = jnp.float32
BF16 = jnp.bfloat16
VMEM = pl.BlockSpec(memory_space=pltpu.VMEM)
SMEM = pl.BlockSpec(memory_space=pltpu.SMEM)
HBM = pl.BlockSpec(memory_space=pltpu.HBM)
ANY = pl.BlockSpec(memory_space=pl.ANY)


def call(kernel, name, specs, shape, dtype, *args, scratch=(), out=VMEM):
    return pl.pallas_call(
        kernel,
        in_specs=specs,
        out_specs=out,
        out_shape=jax.ShapeDtypeStruct(shape, dtype),
        scratch_shapes=scratch,
        compiler_params=pltpu.CompilerParams(vmem_limit_bytes=12 * 2**20),
        name=name,
    )(*args)


def moved(x, by):
    n = lax.axis_size("z")
    return lax.ppermute(x, "z", [(i, i + by) for i in range(n) if 0 <= i + by < n])


def turned(x, by):
    return lax.ppermute(x, "x", [(i, (i + by) % 4) for i in range(4)])


def swapped(x):
    return lax.ppermute(x, "core", [(0, 1), (1, 0)])


def orbital_kernel(place, occupied, own, right, far, left, sems):
    rows = pl.ds(pl.multiple_of(place[0] * HALF, HALF), HALF)
    copies = []
    for turn, out in enumerate((own, right, far, left)):
        columns = pl.ds(pl.multiple_of(lax.rem(place[1] + turn, 4) * COLS, COLS), COLS)
        copies.append(pltpu.make_async_copy(occupied.at[rows, columns], out, sems.at[turn]))
    for copy in copies:
        copy.start()
    for copy in copies:
        copy.wait()


def integral_kernel(mask, integrals, out):
    for s in range(SPAN):
        tile = integrals[s]
        tile = jnp.where(mask[0, s] != 0, tile, jnp.zeros_like(tile))
        for core in range(2):
            for k in range(4):
                at = k * 32 + core * 16
                for x in range(4):
                    out[x, core, s, k * 16 : k * 16 + 16, :] = tile[at : at + 16]


def half_kernel(core, tiles, below2, below, plane, above, above2, first, second, half, window, sems):
    c = core[0]
    moves = ((first, 4, 3, 0), (second, 0, 4, 3), (first, 0, 4, 7), (second, 4, 4, 11), (first, 7, 3, 15))
    copies = [
        pltpu.make_async_copy(part.at[pl.ds(at, n)], window.at[pl.ds(to, n), 1 - c], sems.at[i])
        for i, (part, at, n, to) in enumerate(moves)
    ]
    for copy in copies:
        copy.start()
    at = 0
    for part in (below2, below, plane, above, above2):
        for b in range(part.shape[0]):
            window[at, c] = part[b]
            at += 1
    for copy in copies:
        copy.wait()
    for a in range(4):
        near = window[a : a + SPAN].reshape(SPAN * ROWS, COLS)
        wide = jnp.concatenate(
            [tiles[2 * a : 2 * a + 2, s].reshape(2 * HALF, ROWS) for s in range(SPAN)], 1
        )
        made = jnp.dot(wide, near, preferred_element_type=F32).astype(BF16)
        half[a * HALF : (a + 1) * HALF, :COLS] = made[:HALF]
        half[a * HALF : (a + 1) * HALF, COLS:] = made[HALF:]


def dot_t(a, b):
    return lax.dot_general(a, b, (((1,), (1,)), ((), ())), preferred_element_type=F32)


def interleave(c, mine, other, wide, at):
    for k in range(16):
        to = at + k * 32
        rows = slice(k * 16, k * 16 + 16)
        wide[pl.ds(pl.multiple_of(to + c * 16, 16), 16), :] = mine[rows, :]
        wide[pl.ds(pl.multiple_of(to + 16 - c * 16, 16), 16), :] = other[rows, :]


def tile_kernel(core, up, own, down, up2, own2, down2, out, wide):
    for i, (mine, other) in enumerate(((up, up2), (own, own2), (down, down2))):
        interleave(core[0], mine, other, wide, i * 512)
    for i in range(3):
        out[:, i * 512 : (i + 1) * 512] = dot_t(own[...], wide[i * 512 : (i + 1) * 512, :]).astype(BF16)
    for x in range(4):
        rows = slice(x * HALF, (x + 1) * HALF)
        cut = 1536 + x * ROWS
        if x > 0:
            out[rows, 1536:cut] = dot_t(up[rows, :], wide[1024 : 1024 + x * ROWS, :]).astype(BF16)
        if x < 3:
            out[rows, cut:] = dot_t(down[rows, :], wide[(x + 1) * ROWS : 512, :]).astype(BF16)


def sum_kernel(parts, out):
    for t in range(SPAN):
        total = parts[0, :, t * ROWS : (t + 1) * ROWS].astype(F32)
        for k in range(1, 16):
            total += parts[k, :, t * ROWS : (t + 1) * ROWS].astype(F32)
        out[t] = total


def per_device(occupied, integrals, pair_mask):
    x = lax.axis_index("x")
    c = lax.axis_index("core")
    core = c[None]

    tiles = call(
        integral_kernel, "cut_integrals", [SMEM, VMEM], (4, 2, SPAN, HALF, ROWS), BF16,
        pair_mask, integrals[0, 0],
    )
    tiles, occupied = lax.optimization_barrier((tiles, occupied))
    tiles = lax.all_to_all(tiles.reshape(8, SPAN, HALF, ROWS), ("x", "core"), 0, 0)

    piece = jax.ShapeDtypeStruct((HALF, COLS), BF16)
    mine, right, far, left = pl.pallas_call(
        orbital_kernel,
        in_specs=[SMEM, ANY],
        out_specs=[ANY] * 4,
        out_shape=[piece] * 4,
        scratch_shapes=[pltpu.SemaphoreType.DMA((4,))],
        name="cut_orbitals",
    )(jnp.stack([c, x]), occupied)
    from_left = turned(right, 1)
    from_right = turned(left, -1)
    from_far = turned(far, 2)
    by_turn = jnp.stack([mine, from_right, from_far, from_left] * 2)
    plane = lax.dynamic_slice_in_dim(by_turn, 4 - x, 4, 0)

    below2 = moved(plane[1:], 2)
    above2 = moved(plane[:3], -2)
    below = moved(plane, 1)
    above = moved(plane, -1)
    tiles, above2 = lax.optimization_barrier((tiles, above2))
    first = swapped(jnp.concatenate([plane, below2, above2]))
    second = swapped(jnp.concatenate([below, above]))

    own = call(
        half_kernel, "make_half", [SMEM] + [VMEM] * 6 + [ANY] * 2, (4 * HALF, 2 * COLS), BF16,
        core, tiles, below2, below, plane, above, above2, first, second,
        scratch=[pltpu.VMEM((18, 2, HALF, COLS), BF16), pltpu.SemaphoreType.DMA((5,))],
    )

    up = moved(own, 1)
    down = moved(own, -1)
    own2 = swapped(own)
    partial = call(
        tile_kernel, "make_tiles", [SMEM] + [VMEM] * 6, (256, SPAN * ROWS), BF16,
        core, up, own, down, swapped(up), own2, swapped(down),
        scratch=[pltpu.VMEM((1536, 2 * COLS), BF16)],
    )
    partial = lax.all_to_all(partial.reshape(16, 16, SPAN * ROWS), ("x", "y"), 0, 0)
    total = call(sum_kernel, "sum_parts", [VMEM], (SPAN, 16, ROWS), F32, partial)
    far = total[12:]
    line = jnp.concatenate([moved(far, 1), total[:12], moved(far, -1)], 0)
    out = lax.dynamic_slice_in_dim(line, x, SPAN, 0)
    return (out * pair_mask[0].astype(F32)[:, None, None])[None]


def solution(mesh):
    split = Mesh(mesh.devices.reshape(4, 2, 16, 4), ("y", "core", "z", "x"))
    aux, orb = ("y", "core"), ("z", "x")
    return jax.shard_map(
        per_device,
        mesh=split,
        in_specs=(P(orb, None), P(aux, orb, None, None, None), P(orb, None)),
        out_specs=P(orb, None, aux, None),
        check_vma=False,
    )
```

```python
import jax
import jax.numpy as jnp
from jax import lax
from jax.experimental import pallas as pl
from jax.experimental.pallas import tpu as pltpu
from jax.sharding import Mesh, PartitionSpec as P

ROWS = 128
HALF = 64
COLS = 512
SPAN = 15
F32 = jnp.float32
BF16 = jnp.bfloat16
VMEM = pl.BlockSpec(memory_space=pltpu.VMEM)
SMEM = pl.BlockSpec(memory_space=pltpu.SMEM)
HBM = pl.BlockSpec(memory_space=pltpu.HBM)
ANY = pl.BlockSpec(memory_space=pl.ANY)


def call(kernel, name, specs, shape, dtype, *args, scratch=(), out=VMEM):
    return pl.pallas_call(
        kernel,
        in_specs=specs,
        out_specs=out,
        out_shape=jax.ShapeDtypeStruct(shape, dtype),
        scratch_shapes=scratch,
        compiler_params=pltpu.CompilerParams(vmem_limit_bytes=12 * 2**20),
        name=name,
    )(*args)


def moved(x, by):
    n = lax.axis_size("z")
    return lax.ppermute(x, "z", [(i, i + by) for i in range(n) if 0 <= i + by < n])


def swapped(x):
    return lax.ppermute(x, "core", [(0, 1), (1, 0)])


def orbital_kernel(core, occupied, out, sems):
    rows = pl.ds(pl.multiple_of(core[0] * HALF, HALF), HALF)
    copies = [
        pltpu.make_async_copy(occupied.at[rows, pl.ds(x * COLS, COLS)], out.at[x], sems.at[x])
        for x in range(4)
    ]
    for copy in copies:
        copy.start()
    for copy in copies:
        copy.wait()


def integral_kernel(mask, integrals, out):
    for s in range(SPAN):
        tile = integrals[s]
        tile = jnp.where(mask[0, s] != 0, tile, jnp.zeros_like(tile))
        for core in range(2):
            for k in range(4):
                at = k * 32 + core * 16
                for x in range(4):
                    out[x, core, s, k * 16 : k * 16 + 16, :] = tile[at : at + 16]


def half_kernel(core, tiles, below2, below, plane, above, above2, first, second, half, window, sems):
    c = core[0]
    moves = ((first, 4, 3, 0), (second, 0, 4, 3), (first, 0, 4, 7), (second, 4, 4, 11), (first, 7, 3, 15))
    copies = [
        pltpu.make_async_copy(part.at[pl.ds(at, n)], window.at[pl.ds(to, n), 1 - c], sems.at[i])
        for i, (part, at, n, to) in enumerate(moves)
    ]
    for copy in copies:
        copy.start()
    at = 0
    for part in (below2, below, plane, above, above2):
        for b in range(part.shape[0]):
            window[at, c] = part[b]
            at += 1
    for copy in copies:
        copy.wait()
    for a in range(4):
        near = window[a : a + SPAN].reshape(SPAN * ROWS, COLS)
        wide = jnp.concatenate(
            [tiles[2 * a : 2 * a + 2, s].reshape(2 * HALF, ROWS) for s in range(SPAN)], 1
        )
        made = jnp.dot(wide, near, preferred_element_type=F32).astype(BF16)
        half[a * HALF : (a + 1) * HALF, :COLS] = made[:HALF]
        half[a * HALF : (a + 1) * HALF, COLS:] = made[HALF:]


def dot_t(a, b):
    return lax.dot_general(a, b, (((1,), (1,)), ((), ())), preferred_element_type=F32)


def interleave(c, mine, other, wide, at):
    for k in range(16):
        to = at + k * 32
        rows = slice(k * 16, k * 16 + 16)
        wide[pl.ds(pl.multiple_of(to + c * 16, 16), 16), :] = mine[rows, :]
        wide[pl.ds(pl.multiple_of(to + 16 - c * 16, 16), 16), :] = other[rows, :]


def tile_kernel(core, up, own, down, up2, own2, down2, out, wide):
    for i, (mine, other) in enumerate(((up, up2), (own, own2), (down, down2))):
        interleave(core[0], mine, other, wide, i * 512)
    for i in range(3):
        out[:, i * 512 : (i + 1) * 512] = dot_t(own[...], wide[i * 512 : (i + 1) * 512, :]).astype(BF16)
    for x in range(4):
        rows = slice(x * HALF, (x + 1) * HALF)
        cut = 1536 + x * ROWS
        if x > 0:
            out[rows, 1536:cut] = dot_t(up[rows, :], wide[1024 : 1024 + x * ROWS, :]).astype(BF16)
        if x < 3:
            out[rows, cut:] = dot_t(down[rows, :], wide[(x + 1) * ROWS : 512, :]).astype(BF16)


def sum_kernel(parts, out):
    for t in range(SPAN):
        total = parts[0, :, t * ROWS : (t + 1) * ROWS].astype(F32)
        for k in range(1, 16):
            total += parts[k, :, t * ROWS : (t + 1) * ROWS].astype(F32)
        out[t] = total


def per_device(occupied, integrals, pair_mask):
    x = lax.axis_index("x")
    c = lax.axis_index("core")
    core = c[None]

    pieces = call(
        orbital_kernel, "cut_orbitals", [SMEM, HBM], (4, HALF, COLS), BF16, core, occupied,
        scratch=[pltpu.SemaphoreType.DMA((4,))], out=HBM,
    )
    plane = lax.all_to_all(pieces, "x", 0, 0)

    tiles = call(
        integral_kernel, "cut_integrals", [SMEM, VMEM], (4, 2, SPAN, HALF, ROWS), BF16,
        pair_mask, integrals[0, 0],
    )
    tiles = lax.all_to_all(tiles.reshape(8, SPAN, HALF, ROWS), ("x", "core"), 0, 0)

    below2 = moved(plane[1:], 2)
    above2 = moved(plane[:3], -2)
    below = moved(plane, 1)
    above = moved(plane, -1)
    first = swapped(jnp.concatenate([plane, below2, above2]))
    second = swapped(jnp.concatenate([below, above]))

    own = call(
        half_kernel, "make_half", [SMEM] + [VMEM] * 6 + [ANY] * 2, (4 * HALF, 2 * COLS), BF16,
        core, tiles, below2, below, plane, above, above2, first, second,
        scratch=[pltpu.VMEM((18, 2, HALF, COLS), BF16), pltpu.SemaphoreType.DMA((5,))],
    )

    up = moved(own, 1)
    down = moved(own, -1)
    own2 = swapped(own)
    partial = call(
        tile_kernel, "make_tiles", [SMEM] + [VMEM] * 6, (256, SPAN * ROWS), BF16,
        core, up, own, down, swapped(up), own2, swapped(down),
        scratch=[pltpu.VMEM((1536, 2 * COLS), BF16)],
    )
    partial = lax.all_to_all(partial.reshape(16, 16, SPAN * ROWS), ("x", "y"), 0, 0)
    total = call(sum_kernel, "sum_parts", [VMEM], (SPAN, 16, ROWS), F32, partial)
    far = total[12:]
    line = jnp.concatenate([moved(far, 1), total[:12], moved(far, -1)], 0)
    out = lax.dynamic_slice_in_dim(line, x, SPAN, 0)
    return (out * pair_mask[0].astype(F32)[:, None, None])[None]


def solution(mesh):
    split = Mesh(mesh.devices.reshape(4, 2, 16, 4), ("y", "core", "z", "x"))
    aux, orb = ("y", "core"), ("z", "x")
    return jax.shard_map(
        per_device,
        mesh=split,
        in_specs=(P(orb, None), P(aux, orb, None, None, None), P(orb, None)),
        out_specs=P(orb, None, aux, None),
        check_vma=False,
    )
```

```python
import jax
import jax.numpy as jnp
from jax import lax
from jax.experimental import pallas as pl
from jax.experimental.pallas import tpu as pltpu
from jax.sharding import Mesh, PartitionSpec as P

ROWS = 128
HALF = 64
COLS = 512
SPAN = 15
F32 = jnp.float32
BF16 = jnp.bfloat16
VMEM = pl.BlockSpec(memory_space=pltpu.VMEM)
SMEM = pl.BlockSpec(memory_space=pltpu.SMEM)
HBM = pl.BlockSpec(memory_space=pltpu.HBM)
ANY = pl.BlockSpec(memory_space=pl.ANY)


def call(kernel, name, specs, shape, dtype, *args, scratch=(), out=VMEM):
    return pl.pallas_call(
        kernel,
        in_specs=specs,
        out_specs=out,
        out_shape=jax.ShapeDtypeStruct(shape, dtype),
        scratch_shapes=scratch,
        compiler_params=pltpu.CompilerParams(vmem_limit_bytes=12 * 2**20),
        name=name,
    )(*args)


def moved(x, by):
    n = lax.axis_size("z")
    return lax.ppermute(x, "z", [(i, i + by) for i in range(n) if 0 <= i + by < n])


def swapped(x):
    return lax.ppermute(x, "core", [(0, 1), (1, 0)])


def orbital_kernel(core, occupied, out, sems):
    rows = pl.ds(pl.multiple_of(core[0] * HALF, HALF), HALF)
    copies = [
        pltpu.make_async_copy(occupied.at[rows, pl.ds(x * COLS, COLS)], out.at[x], sems.at[x])
        for x in range(4)
    ]
    for copy in copies:
        copy.start()
    for copy in copies:
        copy.wait()


def integral_kernel(mask, integrals, out):
    for s in range(SPAN):
        tile = integrals[s]
        tile = jnp.where(mask[0, s] != 0, tile, jnp.zeros_like(tile))
        for core in range(2):
            for k in range(4):
                at = k * 32 + core * 16
                for x in range(4):
                    out[x, core, s, k * 16 : k * 16 + 16, :] = tile[at : at + 16]


def window_kernel(core, below2, below, plane, above, above2, first, second, window):
    c = core[0]
    others = ((first, 4), (second, 0), (first, 0), (second, 4), (first, 7))
    at = 0
    for part, (other, start) in zip((below2, below, plane, above, above2), others):
        for b in range(part.shape[0]):
            window[at, c] = part[b]
            window[at, 1 - c] = other[start + b]
            at += 1


def half_kernel(gathered, window, half, tiles, sems):
    copies = [
        pltpu.make_async_copy(gathered.at[pl.ds(2 * a, 2)], tiles.at[pl.ds(2 * a, 2)], sems.at[a])
        for a in range(4)
    ]
    for copy in copies:
        copy.start()
    for a in range(4):
        copies[a].wait()
        near = window[a : a + SPAN].reshape(SPAN * ROWS, COLS)
        wide = jnp.concatenate(
            [tiles[2 * a : 2 * a + 2, s].reshape(2 * HALF, ROWS) for s in range(SPAN)], 1
        )
        made = jnp.dot(wide, near, preferred_element_type=F32).astype(BF16)
        half[a * HALF : (a + 1) * HALF, :COLS] = made[:HALF]
        half[a * HALF : (a + 1) * HALF, COLS:] = made[HALF:]


def dot_t(a, b):
    return lax.dot_general(a, b, (((1,), (1,)), ((), ())), preferred_element_type=F32)


def interleave(c, mine, other, wide, at):
    for k in range(16):
        to = at + k * 32
        rows = slice(k * 16, k * 16 + 16)
        wide[pl.ds(pl.multiple_of(to + c * 16, 16), 16), :] = mine[rows, :]
        wide[pl.ds(pl.multiple_of(to + 16 - c * 16, 16), 16), :] = other[rows, :]


def tile_kernel(core, up, own, down, up2, own2, down2, out, wide):
    for i, (mine, other) in enumerate(((up, up2), (own, own2), (down, down2))):
        interleave(core[0], mine, other, wide, i * 512)
    for i in range(3):
        out[:, i * 512 : (i + 1) * 512] = dot_t(own[...], wide[i * 512 : (i + 1) * 512, :]).astype(BF16)
    for x in range(4):
        rows = slice(x * HALF, (x + 1) * HALF)
        cut = 1536 + x * ROWS
        if x > 0:
            out[rows, 1536:cut] = dot_t(up[rows, :], wide[1024 : 1024 + x * ROWS, :]).astype(BF16)
        if x < 3:
            out[rows, cut:] = dot_t(down[rows, :], wide[(x + 1) * ROWS : 512, :]).astype(BF16)


def sum_kernel(parts, out):
    for t in range(SPAN):
        total = parts[0, :, t * ROWS : (t + 1) * ROWS].astype(F32)
        for k in range(1, 16):
            total += parts[k, :, t * ROWS : (t + 1) * ROWS].astype(F32)
        out[t] = total


def per_device(occupied, integrals, pair_mask):
    x = lax.axis_index("x")
    c = lax.axis_index("core")
    core = c[None]

    pieces = call(
        orbital_kernel, "cut_orbitals", [SMEM, HBM], (4, HALF, COLS), BF16, core, occupied,
        scratch=[pltpu.SemaphoreType.DMA((4,))], out=HBM,
    )
    plane = lax.all_to_all(pieces, "x", 0, 0)

    tiles = call(
        integral_kernel, "cut_integrals", [SMEM, VMEM], (4, 2, SPAN, HALF, ROWS), BF16,
        pair_mask, integrals[0, 0],
    )
    tiles = lax.all_to_all(tiles.reshape(8, SPAN, HALF, ROWS), ("x", "core"), 0, 0)

    below2 = moved(plane[1:], 2)
    above2 = moved(plane[:3], -2)
    below = moved(plane, 1)
    above = moved(plane, -1)
    first = swapped(jnp.concatenate([plane, below2, above2]))
    second = swapped(jnp.concatenate([below, above]))

    window = call(
        window_kernel, "place_orbitals", [SMEM] + [VMEM] * 7, (18, 2, HALF, COLS), BF16,
        core, below2, below, plane, above, above2, first, second,
    )
    own = call(
        half_kernel, "make_half", [ANY, VMEM], (4 * HALF, 2 * COLS), BF16, tiles, window,
        scratch=[pltpu.VMEM((8, SPAN, HALF, ROWS), BF16), pltpu.SemaphoreType.DMA((4,))],
    )

    up = moved(own, 1)
    down = moved(own, -1)
    own2 = swapped(own)
    partial = call(
        tile_kernel, "make_tiles", [SMEM] + [VMEM] * 6, (256, SPAN * ROWS), BF16,
        core, up, own, down, swapped(up), own2, swapped(down),
        scratch=[pltpu.VMEM((1536, 2 * COLS), BF16)],
    )
    partial = lax.all_to_all(partial.reshape(16, 16, SPAN * ROWS), ("x", "y"), 0, 0)
    total = call(sum_kernel, "sum_parts", [VMEM], (SPAN, 16, ROWS), F32, partial)
    far = total[12:]
    line = jnp.concatenate([moved(far, 1), total[:12], moved(far, -1)], 0)
    out = lax.dynamic_slice_in_dim(line, x, SPAN, 0)
    return (out * pair_mask[0].astype(F32)[:, None, None])[None]


def solution(mesh):
    split = Mesh(mesh.devices.reshape(4, 2, 16, 4), ("y", "core", "z", "x"))
    aux, orb = ("y", "core"), ("z", "x")
    return jax.shard_map(
        per_device,
        mesh=split,
        in_specs=(P(orb, None), P(aux, orb, None, None, None), P(orb, None)),
        out_specs=P(orb, None, aux, None),
        check_vma=False,
    )
```

```python
import jax
import jax.numpy as jnp
from jax import lax
from jax.experimental import pallas as pl
from jax.experimental.pallas import tpu as pltpu
from jax.sharding import Mesh, PartitionSpec as P

ROWS = 128
HALF = 64
COLS = 512
SPAN = 15
F32 = jnp.float32
BF16 = jnp.bfloat16
VMEM = pl.BlockSpec(memory_space=pltpu.VMEM)
SMEM = pl.BlockSpec(memory_space=pltpu.SMEM)
HBM = pl.BlockSpec(memory_space=pltpu.HBM)
ANY = pl.BlockSpec(memory_space=pl.ANY)


def call(kernel, name, specs, shape, dtype, *args, scratch=(), out=VMEM):
    return pl.pallas_call(
        kernel,
        in_specs=specs,
        out_specs=out,
        out_shape=jax.ShapeDtypeStruct(shape, dtype),
        scratch_shapes=scratch,
        compiler_params=pltpu.CompilerParams(vmem_limit_bytes=12 * 2**20),
        name=name,
    )(*args)


def moved(x, by):
    n = lax.axis_size("z")
    return lax.ppermute(x, "z", [(i, i + by) for i in range(n) if 0 <= i + by < n])


def turned(x, by):
    return lax.ppermute(x, "x", [(i, (i + by) % 4) for i in range(4)])


def swapped(x):
    return lax.ppermute(x, "core", [(0, 1), (1, 0)])


def sided(x, by):
    n = lax.axis_size("z")
    pairs = [(i, i + by) for i in range(n - by)]
    pairs += [(n + i + by, n + i) for i in range(n - by)]
    return lax.ppermute(x, ("core", "z"), pairs)


def orbital_kernel(occupied, out):
    for x in range(4):
        out[x] = occupied[:, x * COLS : (x + 1) * COLS]


def integral_kernel(core, mask, integrals, keep, give):
    c = core[0]
    for s in range(SPAN):
        kept = mask[0, s] != 0
        for k in range(4):
            for out, shift in ((keep, c * 16), (give, 16 - c * 16)):
                rows = integrals[s, pl.ds(pl.multiple_of(k * 32 + shift, 16), 16), :]
                out[s, k * 16 : k * 16 + 16, :] = jnp.where(kept, rows, jnp.zeros_like(rows))


def half_kernel(place, near, left, right, far, plane, mine, other, half, window):
    c, x = place[0], place[1]
    for b in range(4):
        window[7 + b] = plane[b]
        window[3 + c * 8 + b] = mine[3 + b]
        window[11 - c * 8 + b] = other[3 + b]
    for b in range(3):
        window[c * 15 + b] = mine[b]
        window[15 - c * 15 + b] = other[b]
    own = pl.ds(pl.multiple_of(c * COLS, COLS), COLS)
    rest = pl.ds(pl.multiple_of(COLS - c * COLS, COLS), COLS)
    for turn, tiles in enumerate((near, right, far, left)):
        a = lax.rem(x + turn, 4)
        blocks = window[pl.ds(a, SPAN)].reshape(SPAN * ROWS, COLS)
        wide = jnp.concatenate([tiles[:, s].reshape(2 * HALF, ROWS) for s in range(SPAN)], 1)
        made = jnp.dot(wide, blocks, preferred_element_type=F32).astype(BF16)
        to = pl.ds(pl.multiple_of(a * HALF, HALF), HALF)
        half[to, own] = made[:HALF]
        half[to, rest] = made[HALF:]


def dot_t(a, b):
    return lax.dot_general(a, b, (((1,), (1,)), ((), ())), preferred_element_type=F32)


def interleave(c, mine, other, wide, at):
    for k in range(16):
        to = at + k * 32
        rows = slice(k * 16, k * 16 + 16)
        wide[pl.ds(pl.multiple_of(to + c * 16, 16), 16), :] = mine[rows, :]
        wide[pl.ds(pl.multiple_of(to + 16 - c * 16, 16), 16), :] = other[rows, :]


def tile_kernel(core, up, own, down, up2, own2, down2, out, wide):
    for i, (mine, other) in enumerate(((up, up2), (own, own2), (down, down2))):
        interleave(core[0], mine, other, wide, i * 512)
    for i in range(3):
        out[:, i * 512 : (i + 1) * 512] = dot_t(own[...], wide[i * 512 : (i + 1) * 512, :]).astype(BF16)
    for x in range(4):
        rows = slice(x * HALF, (x + 1) * HALF)
        cut = 1536 + x * ROWS
        if x > 0:
            out[rows, 1536:cut] = dot_t(up[rows, :], wide[1024 : 1024 + x * ROWS, :]).astype(BF16)
        if x < 3:
            out[rows, cut:] = dot_t(down[rows, :], wide[(x + 1) * ROWS : 512, :]).astype(BF16)


def sum_kernel(parts, out):
    for t in range(SPAN):
        total = parts[0, :, t * ROWS : (t + 1) * ROWS].astype(F32)
        for k in range(1, 16):
            total += parts[k, :, t * ROWS : (t + 1) * ROWS].astype(F32)
        out[t] = total


def per_device(occupied, integrals, pair_mask):
    x = lax.axis_index("x")
    c = lax.axis_index("core")
    core = c[None]

    pieces = call(orbital_kernel, "cut_orbitals", [VMEM], (4, ROWS, COLS), BF16, occupied)
    plane = lax.all_to_all(pieces, "x", 0, 0)

    rows = jax.ShapeDtypeStruct((SPAN, HALF, ROWS), BF16)
    keep, give = pl.pallas_call(
        integral_kernel,
        in_specs=[SMEM, SMEM, VMEM],
        out_specs=[VMEM] * 2,
        out_shape=[rows] * 2,
        name="cut_integrals",
    )(core, pair_mask, integrals[0, 0])
    taken = swapped(give)
    near = jnp.stack([keep, taken])
    left = turned(near, 1)
    right = turned(near, -1)
    far = turned(near, 2)

    two_away = sided(lax.dynamic_slice_in_dim(plane, 1 - c, 3, 0), 2)
    one_away = sided(plane, 1)
    two_away, left, right, far = lax.optimization_barrier((two_away, left, right, far))
    mine = jnp.concatenate([two_away, one_away])
    other = swapped(mine)

    own = call(
        half_kernel, "make_half", [SMEM] + [VMEM] * 7, (4 * HALF, 2 * COLS), BF16,
        jnp.stack([c, x]), near, left, right, far, plane, mine, other,
        scratch=[pltpu.VMEM((18, ROWS, COLS), BF16)],
    )

    up = moved(own, 1)
    down = moved(own, -1)
    own2 = swapped(own)
    partial = call(
        tile_kernel, "make_tiles", [SMEM] + [VMEM] * 6, (256, SPAN * ROWS), BF16,
        core, up, own, down, swapped(up), own2, swapped(down),
        scratch=[pltpu.VMEM((1536, 2 * COLS), BF16)],
    )
    partial = lax.all_to_all(partial.reshape(16, 16, SPAN * ROWS), ("x", "y"), 0, 0)
    total = call(sum_kernel, "sum_parts", [VMEM], (SPAN, 16, ROWS), F32, partial)
    far = total[12:]
    line = jnp.concatenate([moved(far, 1), total[:12], moved(far, -1)], 0)
    out = lax.dynamic_slice_in_dim(line, x, SPAN, 0)
    return (out * pair_mask[0].astype(F32)[:, None, None])[None]


def solution(mesh):
    split = Mesh(mesh.devices.reshape(4, 2, 16, 4), ("y", "core", "z", "x"))
    aux, orb = ("y", "core"), ("z", "x")
    return jax.shard_map(
        per_device,
        mesh=split,
        in_specs=(P(orb, None), P(aux, orb, None, None, None), P(orb, None)),
        out_specs=P(orb, None, aux, None),
        check_vma=False,
    )
```

```python
import jax
import jax.numpy as jnp
from jax import lax
from jax.experimental import pallas as pl
from jax.experimental.pallas import tpu as pltpu
from jax.sharding import Mesh, PartitionSpec as P

ROWS = 128
HALF = 64
COLS = 512
SPAN = 15
F32 = jnp.float32
BF16 = jnp.bfloat16
VMEM = pl.BlockSpec(memory_space=pltpu.VMEM)
SMEM = pl.BlockSpec(memory_space=pltpu.SMEM)
HBM = pl.BlockSpec(memory_space=pltpu.HBM)
ANY = pl.BlockSpec(memory_space=pl.ANY)


def call(kernel, name, specs, shape, dtype, *args, scratch=(), out=VMEM):
    return pl.pallas_call(
        kernel,
        in_specs=specs,
        out_specs=out,
        out_shape=jax.ShapeDtypeStruct(shape, dtype),
        scratch_shapes=scratch,
        compiler_params=pltpu.CompilerParams(vmem_limit_bytes=12 * 2**20),
        name=name,
    )(*args)


def moved(x, by):
    n = lax.axis_size("z")
    return lax.ppermute(x, "z", [(i, i + by) for i in range(n) if 0 <= i + by < n])


def swapped(x):
    return lax.ppermute(x, "core", [(0, 1), (1, 0)])


def orbital_kernel(core, occupied, out, sems):
    rows = pl.ds(pl.multiple_of(core[0] * HALF, HALF), HALF)
    copies = [
        pltpu.make_async_copy(occupied.at[rows, pl.ds(x * COLS, COLS)], out.at[x], sems.at[x])
        for x in range(4)
    ]
    for copy in copies:
        copy.start()
    for copy in copies:
        copy.wait()


def integral_kernel(mask, integrals, out):
    for s in range(SPAN):
        tile = integrals[s]
        tile = jnp.where(mask[0, s] != 0, tile, jnp.zeros_like(tile))
        for core in range(2):
            for k in range(4):
                at = k * 32 + core * 16
                for x in range(4):
                    out[core, x, s, k * 16 : k * 16 + 16, :] = tile[at : at + 16]


def window_kernel(core, below2, below, plane, above, above2, first, second, window):
    c = core[0]
    others = ((first, 4), (second, 0), (first, 0), (second, 4), (first, 7))
    at = 0
    for part, (other, start) in zip((below2, below, plane, above, above2), others):
        for b in range(part.shape[0]):
            window[at, c] = part[b]
            window[at, 1 - c] = other[start + b]
            at += 1


def half_kernel(gathered, window, half, tiles, sems):
    copies = [pltpu.make_async_copy(gathered.at[i], tiles.at[i], sems.at[i]) for i in (0, 4, 1, 5, 2, 6, 3, 7)]
    for copy in copies:
        copy.start()
    for a in range(4):
        copies[2 * a].wait()
        copies[2 * a + 1].wait()
        near = window[a : a + SPAN].reshape(SPAN * ROWS, COLS)
        wide = jnp.concatenate(
            [jnp.concatenate([tiles[a, s], tiles[4 + a, s]], 0) for s in range(SPAN)], 1
        )
        made = jnp.dot(wide, near, preferred_element_type=F32).astype(BF16)
        half[a * HALF : (a + 1) * HALF, :COLS] = made[:HALF]
        half[a * HALF : (a + 1) * HALF, COLS:] = made[HALF:]


def dot_t(a, b):
    return lax.dot_general(a, b, (((1,), (1,)), ((), ())), preferred_element_type=F32)


def interleave(c, mine, other, wide, at):
    for k in range(16):
        to = at + k * 32
        rows = slice(k * 16, k * 16 + 16)
        wide[pl.ds(pl.multiple_of(to + c * 16, 16), 16), :] = mine[rows, :]
        wide[pl.ds(pl.multiple_of(to + 16 - c * 16, 16), 16), :] = other[rows, :]


def tile_kernel(core, up, own, down, up2, own2, down2, out, wide):
    for i, (mine, other) in enumerate(((up, up2), (own, own2), (down, down2))):
        interleave(core[0], mine, other, wide, i * 512)

    def put(made, x, at):
        for y in range(4):
            out[y * 4 + x, :, at : at + made.shape[1]] = made[y * 16 : y * 16 + 16].astype(BF16)

    for i in range(3):
        made = dot_t(own[...], wide[i * 512 : (i + 1) * 512, :])
        for x in range(4):
            put(made[x * HALF : (x + 1) * HALF], x, i * 512)
    for x in range(4):
        rows = slice(x * HALF, (x + 1) * HALF)
        if x > 0:
            put(dot_t(up[rows, :], wide[1024 : 1024 + x * ROWS, :]), x, 1536)
        if x < 3:
            put(dot_t(down[rows, :], wide[(x + 1) * ROWS : 512, :]), x, 1536 + x * ROWS)


def sum_kernel(parts, out):
    for t in range(SPAN):
        total = parts[0, :, t * ROWS : (t + 1) * ROWS].astype(F32)
        for k in range(1, 16):
            total += parts[k, :, t * ROWS : (t + 1) * ROWS].astype(F32)
        out[t] = total


def per_device(occupied, integrals, pair_mask):
    x = lax.axis_index("x")
    c = lax.axis_index("core")
    core = c[None]

    pieces = call(
        orbital_kernel, "cut_orbitals", [SMEM, HBM], (4, HALF, COLS), BF16, core, occupied,
        scratch=[pltpu.SemaphoreType.DMA((4,))], out=HBM,
    )
    plane = lax.all_to_all(pieces, "x", 0, 0)

    tiles = call(
        integral_kernel, "cut_integrals", [SMEM, VMEM], (2, 4, SPAN, HALF, ROWS), BF16,
        pair_mask, integrals[0, 0],
    )
    tiles = lax.all_to_all(tiles.reshape(8, SPAN, HALF, ROWS), ("core", "x"), 0, 0)

    below2 = moved(plane[1:], 2)
    above2 = moved(plane[:3], -2)
    below = moved(plane, 1)
    above = moved(plane, -1)
    first = swapped(jnp.concatenate([plane, below2, above2]))
    second = swapped(jnp.concatenate([below, above]))

    window = call(
        window_kernel, "place_orbitals", [SMEM] + [VMEM] * 7, (18, 2, HALF, COLS), BF16,
        core, below2, below, plane, above, above2, first, second,
    )
    own = call(
        half_kernel, "make_half", [ANY, VMEM], (4 * HALF, 2 * COLS), BF16, tiles, window,
        scratch=[pltpu.VMEM((8, SPAN, HALF, ROWS), BF16), pltpu.SemaphoreType.DMA((8,))],
    )

    up = moved(own, 1)
    down = moved(own, -1)
    own2 = swapped(own)
    partial = call(
        tile_kernel, "make_tiles", [SMEM] + [VMEM] * 6, (16, 16, SPAN * ROWS), BF16,
        core, up, own, down, swapped(up), own2, swapped(down),
        scratch=[pltpu.VMEM((1536, 2 * COLS), BF16)],
    )
    partial = lax.all_to_all(partial, ("y", "x"), 0, 0)
    total = call(sum_kernel, "sum_parts", [VMEM], (SPAN, 16, ROWS), F32, partial)
    far = total[12:]
    line = jnp.concatenate([moved(far, 1), total[:12], moved(far, -1)], 0)
    out = lax.dynamic_slice_in_dim(line, x, SPAN, 0)
    return (out * pair_mask[0].astype(F32)[:, None, None])[None]


def solution(mesh):
    split = Mesh(mesh.devices.reshape(4, 2, 16, 4), ("y", "core", "z", "x"))
    aux, orb = ("y", "core"), ("z", "x")
    return jax.shard_map(
        per_device,
        mesh=split,
        in_specs=(P(orb, None), P(aux, orb, None, None, None), P(orb, None)),
        out_specs=P(orb, None, aux, None),
        check_vma=False,
    )
```

```python
import jax
import jax.numpy as jnp
from jax import lax
from jax.experimental import pallas as pl
from jax.experimental.pallas import tpu as pltpu
from jax.sharding import Mesh, PartitionSpec as P

ROWS = 128
HALF = 64
COLS = 512
SPAN = 15
F32 = jnp.float32
BF16 = jnp.bfloat16
VMEM = pl.BlockSpec(memory_space=pltpu.VMEM)
SMEM = pl.BlockSpec(memory_space=pltpu.SMEM)
HBM = pl.BlockSpec(memory_space=pltpu.HBM)
ANY = pl.BlockSpec(memory_space=pl.ANY)


def call(kernel, name, specs, shape, dtype, *args, scratch=(), out=VMEM):
    return pl.pallas_call(
        kernel,
        in_specs=specs,
        out_specs=out,
        out_shape=jax.ShapeDtypeStruct(shape, dtype),
        scratch_shapes=scratch,
        compiler_params=pltpu.CompilerParams(vmem_limit_bytes=12 * 2**20),
        name=name,
    )(*args)


def moved(x, by):
    n = lax.axis_size("z")
    return lax.ppermute(x, "z", [(i, i + by) for i in range(n) if 0 <= i + by < n])


def swapped(x):
    return lax.ppermute(x, "core", [(0, 1), (1, 0)])


def orbital_kernel(core, occupied, out, sems):
    rows = pl.ds(pl.multiple_of(core[0] * HALF, HALF), HALF)
    copies = [
        pltpu.make_async_copy(occupied.at[rows, pl.ds(x * COLS, COLS)], out.at[x], sems.at[x])
        for x in range(4)
    ]
    for copy in copies:
        copy.start()
    for copy in copies:
        copy.wait()


def integral_kernel(mask, integrals, out):
    for s in range(SPAN):
        tile = integrals[s]
        tile = jnp.where(mask[0, s] != 0, tile, jnp.zeros_like(tile))
        for core in range(2):
            for k in range(4):
                at = k * 32 + core * 16
                for x in range(4):
                    out[x, core, s, k * 16 : k * 16 + 16, :] = tile[at : at + 16]


def half_kernel(core, tiles, below2, below, plane, above, above2, first, second, half, window, sems):
    c = core[0]
    moves = ((first, 4, 3, 0), (second, 0, 4, 3), (first, 0, 4, 7), (second, 4, 4, 11), (first, 7, 3, 15))
    copies = [
        pltpu.make_async_copy(part.at[pl.ds(at, n)], window.at[pl.ds(to, n), 1 - c], sems.at[i])
        for i, (part, at, n, to) in enumerate(moves)
    ]
    for copy in copies:
        copy.start()
    at = 0
    for part in (below2, below, plane, above, above2):
        for b in range(part.shape[0]):
            window[at, c] = part[b]
            at += 1
    for copy in copies:
        copy.wait()
    for a in range(4):
        near = window[a : a + SPAN].reshape(SPAN * ROWS, COLS)
        wide = jnp.concatenate(
            [tiles[2 * a : 2 * a + 2, s].reshape(2 * HALF, ROWS) for s in range(SPAN)], 1
        )
        made = jnp.dot(wide, near, preferred_element_type=F32).astype(BF16)
        half[a * HALF : (a + 1) * HALF, :COLS] = made[:HALF]
        half[a * HALF : (a + 1) * HALF, COLS:] = made[HALF:]


def dot_t(a, b):
    return lax.dot_general(a, b, (((1,), (1,)), ((), ())), preferred_element_type=F32)


def interleave(c, mine, other, wide, at):
    for k in range(16):
        to = at + k * 32
        rows = slice(k * 16, k * 16 + 16)
        wide[pl.ds(pl.multiple_of(to + c * 16, 16), 16), :] = mine[rows, :]
        wide[pl.ds(pl.multiple_of(to + 16 - c * 16, 16), 16), :] = other[rows, :]


def near_kernel(core, up, own, up2, own2, out, wide):
    interleave(core[0], up, up2, wide, 0)
    interleave(core[0], own, own2, wide, 512)
    for i in range(2):
        out[:, i * 512 : (i + 1) * 512] = dot_t(own[...], wide[i * 512 : (i + 1) * 512, :]).astype(BF16)


def tile_kernel(core, near, up, own, down, up2, down2, out, wide):
    interleave(core[0], up, up2, wide, 0)
    interleave(core[0], down, down2, wide, 512)
    out[:, :1024] = near[...]
    out[:, 1024:1536] = dot_t(own[...], wide[512:1024, :]).astype(BF16)
    for x in range(4):
        rows = slice(x * HALF, (x + 1) * HALF)
        cut = 1536 + x * ROWS
        if x > 0:
            out[rows, 1536:cut] = dot_t(up[rows, :], wide[512 : 512 + x * ROWS, :]).astype(BF16)
        if x < 3:
            out[rows, cut:] = dot_t(down[rows, :], wide[(x + 1) * ROWS : 512, :]).astype(BF16)


def sum_kernel(parts, out):
    for t in range(SPAN):
        total = parts[0, :, t * ROWS : (t + 1) * ROWS].astype(F32)
        for k in range(1, 16):
            total += parts[k, :, t * ROWS : (t + 1) * ROWS].astype(F32)
        out[t] = total


def per_device(occupied, integrals, pair_mask):
    x = lax.axis_index("x")
    c = lax.axis_index("core")
    core = c[None]

    pieces = call(
        orbital_kernel, "cut_orbitals", [SMEM, HBM], (4, HALF, COLS), BF16, core, occupied,
        scratch=[pltpu.SemaphoreType.DMA((4,))], out=HBM,
    )
    plane = lax.all_to_all(pieces, "x", 0, 0)

    tiles = call(
        integral_kernel, "cut_integrals", [SMEM, VMEM], (4, 2, SPAN, HALF, ROWS), BF16,
        pair_mask, integrals[0, 0],
    )
    tiles = lax.all_to_all(tiles.reshape(8, SPAN, HALF, ROWS), ("x", "core"), 0, 0)

    below2 = moved(plane[1:], 2)
    above2 = moved(plane[:3], -2)
    below = moved(plane, 1)
    above = moved(plane, -1)
    first = swapped(jnp.concatenate([plane, below2, above2]))
    tiles, above = lax.optimization_barrier((tiles, above))
    second = swapped(jnp.concatenate([below, above]))

    own = call(
        half_kernel, "make_half", [SMEM] + [VMEM] * 6 + [ANY] * 2, (4 * HALF, 2 * COLS), BF16,
        core, tiles, below2, below, plane, above, above2, first, second,
        scratch=[pltpu.VMEM((18, 2, HALF, COLS), BF16), pltpu.SemaphoreType.DMA((5,))],
    )

    up = moved(own, 1)
    down = moved(own, -1)
    own2 = swapped(own)
    up2 = swapped(up)
    near = call(
        near_kernel, "make_near", [SMEM] + [VMEM] * 4, (256, 1024), BF16, core, up, own, up2, own2,
        scratch=[pltpu.VMEM((1024, 2 * COLS), BF16)],
    )
    partial = call(
        tile_kernel, "make_tiles", [SMEM] + [VMEM] * 6, (256, SPAN * ROWS), BF16,
        core, near, up, own, down, up2, swapped(down),
        scratch=[pltpu.VMEM((1024, 2 * COLS), BF16)],
    )
    partial = lax.all_to_all(partial.reshape(16, 16, SPAN * ROWS), ("x", "y"), 0, 0)
    total = call(sum_kernel, "sum_parts", [VMEM], (SPAN, 16, ROWS), F32, partial)
    far = total[12:]
    line = jnp.concatenate([moved(far, 1), total[:12], moved(far, -1)], 0)
    out = lax.dynamic_slice_in_dim(line, x, SPAN, 0)
    return (out * pair_mask[0].astype(F32)[:, None, None])[None]


def solution(mesh):
    split = Mesh(mesh.devices.reshape(4, 2, 16, 4), ("y", "core", "z", "x"))
    aux, orb = ("y", "core"), ("z", "x")
    return jax.shard_map(
        per_device,
        mesh=split,
        in_specs=(P(orb, None), P(aux, orb, None, None, None), P(orb, None)),
        out_specs=P(orb, None, aux, None),
        check_vma=False,
    )
```

```python
import jax
import jax.numpy as jnp
from jax import lax
from jax.experimental import pallas as pl
from jax.experimental.pallas import tpu as pltpu
from jax.sharding import Mesh, PartitionSpec as P

ROWS = 128
HALF = 64
COLS = 512
SPAN = 15
F32 = jnp.float32
BF16 = jnp.bfloat16
VMEM = pl.BlockSpec(memory_space=pltpu.VMEM)
SMEM = pl.BlockSpec(memory_space=pltpu.SMEM)
HBM = pl.BlockSpec(memory_space=pltpu.HBM)
ANY = pl.BlockSpec(memory_space=pl.ANY)


def call(kernel, name, specs, shape, dtype, *args, scratch=(), out=VMEM):
    return pl.pallas_call(
        kernel,
        in_specs=specs,
        out_specs=out,
        out_shape=jax.ShapeDtypeStruct(shape, dtype),
        scratch_shapes=scratch,
        compiler_params=pltpu.CompilerParams(vmem_limit_bytes=12 * 2**20),
        name=name,
    )(*args)


def moved(x, by):
    n = lax.axis_size("z")
    return lax.ppermute(x, "z", [(i, i + by) for i in range(n) if 0 <= i + by < n])


def swapped(x):
    return lax.ppermute(x, "core", [(0, 1), (1, 0)])


def orbital_kernel(core, occupied, out, sems):
    rows = pl.ds(pl.multiple_of(core[0] * HALF, HALF), HALF)
    copies = [
        pltpu.make_async_copy(occupied.at[rows, pl.ds(x * COLS, COLS)], out.at[x], sems.at[x])
        for x in range(4)
    ]
    for copy in copies:
        copy.start()
    for copy in copies:
        copy.wait()


def integral_kernel(mask, integrals, out):
    for s in range(SPAN):
        tile = integrals[s]
        tile = jnp.where(mask[0, s] != 0, tile, jnp.zeros_like(tile))
        for core in range(2):
            for k in range(4):
                at = k * 32 + core * 16
                for x in range(4):
                    out[core, x, s, k * 16 : k * 16 + 16, :] = tile[at : at + 16]


def half_kernel(core, tiles, below2, below, plane, above, above2, first, second, half, window, sems):
    c = core[0]
    moves = ((first, 4, 3, 0), (second, 0, 4, 3), (first, 0, 4, 7), (second, 4, 4, 11), (first, 7, 3, 15))
    copies = [
        pltpu.make_async_copy(part.at[pl.ds(at, n)], window.at[pl.ds(to, n), 1 - c], sems.at[i])
        for i, (part, at, n, to) in enumerate(moves)
    ]
    for copy in copies:
        copy.start()
    at = 0
    for part in (below2, below, plane, above, above2):
        for b in range(part.shape[0]):
            window[at, c] = part[b]
            at += 1
    for copy in copies:
        copy.wait()
    for a in range(4):
        near = window[a : a + SPAN].reshape(SPAN * ROWS, COLS)
        wide = jnp.concatenate(
            [jnp.concatenate([tiles[a, s], tiles[4 + a, s]], 0) for s in range(SPAN)], 1
        )
        made = jnp.dot(wide, near, preferred_element_type=F32).astype(BF16)
        half[a * HALF : (a + 1) * HALF, :COLS] = made[:HALF]
        half[a * HALF : (a + 1) * HALF, COLS:] = made[HALF:]


def dot_t(a, b):
    return lax.dot_general(a, b, (((1,), (1,)), ((), ())), preferred_element_type=F32)


def interleave(c, mine, other, wide, at):
    for k in range(16):
        to = at + k * 32
        rows = slice(k * 16, k * 16 + 16)
        wide[pl.ds(pl.multiple_of(to + c * 16, 16), 16), :] = mine[rows, :]
        wide[pl.ds(pl.multiple_of(to + 16 - c * 16, 16), 16), :] = other[rows, :]


def near_kernel(core, up, own, up2, own2, out, wide):
    interleave(core[0], up, up2, wide, 0)
    interleave(core[0], own, own2, wide, 512)
    for i in range(2):
        out[:, i * 512 : (i + 1) * 512] = dot_t(own[...], wide[i * 512 : (i + 1) * 512, :]).astype(BF16)


def tile_kernel(core, near, up, own, down, up2, down2, out, wide):
    interleave(core[0], up, up2, wide, 0)
    interleave(core[0], down, down2, wide, 512)
    out[:, :1024] = near[...]
    out[:, 1024:1536] = dot_t(own[...], wide[512:1024, :]).astype(BF16)
    for x in range(4):
        rows = slice(x * HALF, (x + 1) * HALF)
        cut = 1536 + x * ROWS
        if x > 0:
            out[rows, 1536:cut] = dot_t(up[rows, :], wide[512 : 512 + x * ROWS, :]).astype(BF16)
        if x < 3:
            out[rows, cut:] = dot_t(down[rows, :], wide[(x + 1) * ROWS : 512, :]).astype(BF16)


def sum_kernel(parts, out):
    for t in range(SPAN):
        total = parts[0, :, t * ROWS : (t + 1) * ROWS].astype(F32)
        for k in range(1, 16):
            total += parts[k, :, t * ROWS : (t + 1) * ROWS].astype(F32)
        out[t] = total


def per_device(occupied, integrals, pair_mask):
    x = lax.axis_index("x")
    c = lax.axis_index("core")
    core = c[None]

    pieces = call(
        orbital_kernel, "cut_orbitals", [SMEM, HBM], (4, HALF, COLS), BF16, core, occupied,
        scratch=[pltpu.SemaphoreType.DMA((4,))], out=HBM,
    )
    plane = lax.all_to_all(pieces, "x", 0, 0)

    tiles = call(
        integral_kernel, "cut_integrals", [SMEM, VMEM], (2, 4, SPAN, HALF, ROWS), BF16,
        pair_mask, integrals[0, 0],
    )
    tiles = lax.all_to_all(tiles.reshape(8, SPAN, HALF, ROWS), ("core", "x"), 0, 0)

    below2 = moved(plane[1:], 2)
    above2 = moved(plane[:3], -2)
    below = moved(plane, 1)
    above = moved(plane, -1)
    first = swapped(jnp.concatenate([plane, below2, above2]))
    tiles, above = lax.optimization_barrier((tiles, above))
    second = swapped(jnp.concatenate([below, above]))

    own = call(
        half_kernel, "make_half", [SMEM] + [VMEM] * 6 + [ANY] * 2, (4 * HALF, 2 * COLS), BF16,
        core, tiles, below2, below, plane, above, above2, first, second,
        scratch=[pltpu.VMEM((18, 2, HALF, COLS), BF16), pltpu.SemaphoreType.DMA((5,))],
    )

    up = moved(own, 1)
    down = moved(own, -1)
    own2 = swapped(own)
    up2 = swapped(up)
    near = call(
        near_kernel, "make_near", [SMEM] + [VMEM] * 4, (256, 1024), BF16, core, up, own, up2, own2,
        scratch=[pltpu.VMEM((1024, 2 * COLS), BF16)],
    )
    partial = call(
        tile_kernel, "make_tiles", [SMEM] + [VMEM] * 6, (256, SPAN * ROWS), BF16,
        core, near, up, own, down, up2, swapped(down),
        scratch=[pltpu.VMEM((1024, 2 * COLS), BF16)],
    )
    partial = lax.all_to_all(partial.reshape(16, 16, SPAN * ROWS), ("x", "y"), 0, 0)
    total = call(sum_kernel, "sum_parts", [VMEM], (SPAN, 16, ROWS), F32, partial)
    far = total[12:]
    line = jnp.concatenate([moved(far, 1), total[:12], moved(far, -1)], 0)
    out = lax.dynamic_slice_in_dim(line, x, SPAN, 0)
    return (out * pair_mask[0].astype(F32)[:, None, None])[None]


def solution(mesh):
    split = Mesh(mesh.devices.reshape(4, 2, 16, 4), ("y", "core", "z", "x"))
    aux, orb = ("y", "core"), ("z", "x")
    return jax.shard_map(
        per_device,
        mesh=split,
        in_specs=(P(orb, None), P(aux, orb, None, None, None), P(orb, None)),
        out_specs=P(orb, None, aux, None),
        check_vma=False,
    )
```

```python
import jax
import jax.numpy as jnp
from jax import lax
from jax.experimental import pallas as pl
from jax.experimental.pallas import tpu as pltpu
from jax.sharding import Mesh, PartitionSpec as P

ROWS = 128
HALF = 64
COLS = 512
SPAN = 15
F32 = jnp.float32
BF16 = jnp.bfloat16
VMEM = pl.BlockSpec(memory_space=pltpu.VMEM)
SMEM = pl.BlockSpec(memory_space=pltpu.SMEM)
HBM = pl.BlockSpec(memory_space=pltpu.HBM)
ANY = pl.BlockSpec(memory_space=pl.ANY)


def call(kernel, name, specs, shape, dtype, *args, scratch=(), out=VMEM):
    return pl.pallas_call(
        kernel,
        in_specs=specs,
        out_specs=out,
        out_shape=jax.ShapeDtypeStruct(shape, dtype),
        scratch_shapes=scratch,
        compiler_params=pltpu.CompilerParams(vmem_limit_bytes=12 * 2**20),
        name=name,
    )(*args)


def moved(x, by):
    n = lax.axis_size("z")
    return lax.ppermute(x, "z", [(i, i + by) for i in range(n) if 0 <= i + by < n])


def swapped(x):
    return lax.ppermute(x, "core", [(0, 1), (1, 0)])


def orbital_kernel(core, occupied, out, sems):
    rows = pl.ds(pl.multiple_of(core[0] * HALF, HALF), HALF)
    copies = [
        pltpu.make_async_copy(occupied.at[rows, pl.ds(x * COLS, COLS)], out.at[x], sems.at[x])
        for x in range(4)
    ]
    for copy in copies:
        copy.start()
    for copy in copies:
        copy.wait()


def integral_kernel(mask, integrals, out):
    for s in range(SPAN):
        tile = integrals[s]
        tile = jnp.where(mask[0, s] != 0, tile, jnp.zeros_like(tile))
        for core in range(2):
            for k in range(4):
                at = k * 32 + core * 16
                for x in range(4):
                    out[x, core, s, k * 16 : k * 16 + 16, :] = tile[at : at + 16]


def window_kernel(core, below2, below, plane, above, above2, first, second, window):
    c = core[0]
    others = ((first, 4), (second, 0), (first, 0), (second, 4), (first, 7))
    at = 0
    for part, (other, start) in zip((below2, below, plane, above, above2), others):
        for b in range(part.shape[0]):
            window[at, c] = part[b]
            window[at, 1 - c] = other[start + b]
            at += 1


def half_kernel(gathered, window, half, tiles, sems):
    copies = [
        pltpu.make_async_copy(gathered.at[pl.ds(2 * a, 2)], tiles.at[pl.ds(2 * a, 2)], sems.at[a])
        for a in range(4)
    ]
    for copy in copies:
        copy.start()
    for a in range(4):
        copies[a].wait()
        near = window[a : a + SPAN].reshape(SPAN * ROWS, COLS)
        wide = jnp.concatenate(
            [tiles[2 * a : 2 * a + 2, s].reshape(2 * HALF, ROWS) for s in range(SPAN)], 1
        )
        made = jnp.dot(wide, near, preferred_element_type=F32).astype(BF16)
        half[a * HALF : (a + 1) * HALF, :COLS] = made[:HALF]
        half[a * HALF : (a + 1) * HALF, COLS:] = made[HALF:]


def dot_t(a, b):
    return lax.dot_general(a, b, (((1,), (1,)), ((), ())), preferred_element_type=F32)


def interleave(c, mine, other, wide, at):
    for k in range(16):
        to = at + k * 32
        rows = slice(k * 16, k * 16 + 16)
        wide[pl.ds(pl.multiple_of(to + c * 16, 16), 16), :] = mine[rows, :]
        wide[pl.ds(pl.multiple_of(to + 16 - c * 16, 16), 16), :] = other[rows, :]


def near_kernel(core, up, own, up2, own2, out, wide):
    interleave(core[0], up, up2, wide, 0)
    interleave(core[0], own, own2, wide, 512)
    for i in range(2):
        out[:, i * 512 : (i + 1) * 512] = dot_t(own[...], wide[i * 512 : (i + 1) * 512, :]).astype(BF16)


def tile_kernel(core, near, up, own, down, up2, down2, out, wide):
    interleave(core[0], up, up2, wide, 0)
    interleave(core[0], down, down2, wide, 512)
    out[:, :1024] = near[...]
    out[:, 1024:1536] = dot_t(own[...], wide[512:1024, :]).astype(BF16)
    for x in range(4):
        rows = slice(x * HALF, (x + 1) * HALF)
        cut = 1536 + x * ROWS
        if x > 0:
            out[rows, 1536:cut] = dot_t(up[rows, :], wide[512 : 512 + x * ROWS, :]).astype(BF16)
        if x < 3:
            out[rows, cut:] = dot_t(down[rows, :], wide[(x + 1) * ROWS : 512, :]).astype(BF16)


def sum_kernel(parts, out):
    for t in range(SPAN):
        total = parts[0, :, t * ROWS : (t + 1) * ROWS].astype(F32)
        for k in range(1, 16):
            total += parts[k, :, t * ROWS : (t + 1) * ROWS].astype(F32)
        out[t] = total


def per_device(occupied, integrals, pair_mask):
    x = lax.axis_index("x")
    c = lax.axis_index("core")
    core = c[None]

    pieces = call(
        orbital_kernel, "cut_orbitals", [SMEM, HBM], (4, HALF, COLS), BF16, core, occupied,
        scratch=[pltpu.SemaphoreType.DMA((4,))], out=HBM,
    )
    plane = lax.all_to_all(pieces, "x", 0, 0)

    tiles = call(
        integral_kernel, "cut_integrals", [SMEM, VMEM], (4, 2, SPAN, HALF, ROWS), BF16,
        pair_mask, integrals[0, 0],
    )
    tiles = lax.all_to_all(tiles.reshape(8, SPAN, HALF, ROWS), ("x", "core"), 0, 0)

    below2 = moved(plane[1:], 2)
    above2 = moved(plane[:3], -2)
    below = moved(plane, 1)
    above = moved(plane, -1)
    first = swapped(jnp.concatenate([plane, below2, above2]))
    second = swapped(jnp.concatenate([below, above]))

    window = call(
        window_kernel, "place_orbitals", [SMEM] + [VMEM] * 7, (18, 2, HALF, COLS), BF16,
        core, below2, below, plane, above, above2, first, second,
    )
    own = call(
        half_kernel, "make_half", [ANY, VMEM], (4 * HALF, 2 * COLS), BF16, tiles, window,
        scratch=[pltpu.VMEM((8, SPAN, HALF, ROWS), BF16), pltpu.SemaphoreType.DMA((4,))],
    )

    up = moved(own, 1)
    down = moved(own, -1)
    own2 = swapped(own)
    up2 = swapped(up)
    near = call(
        near_kernel, "make_near", [SMEM] + [VMEM] * 4, (256, 1024), BF16, core, up, own, up2, own2,
        scratch=[pltpu.VMEM((1024, 2 * COLS), BF16)],
    )
    partial = call(
        tile_kernel, "make_tiles", [SMEM] + [VMEM] * 6, (256, SPAN * ROWS), BF16,
        core, near, up, own, down, up2, swapped(down),
        scratch=[pltpu.VMEM((1024, 2 * COLS), BF16)],
    )
    partial = lax.all_to_all(partial.reshape(16, 16, SPAN * ROWS), ("x", "y"), 0, 0)
    total = call(sum_kernel, "sum_parts", [VMEM], (SPAN, 16, ROWS), F32, partial)
    far = total[12:]
    line = jnp.concatenate([moved(far, 1), total[:12], moved(far, -1)], 0)
    out = lax.dynamic_slice_in_dim(line, x, SPAN, 0)
    return (out * pair_mask[0].astype(F32)[:, None, None])[None]


def solution(mesh):
    split = Mesh(mesh.devices.reshape(4, 2, 16, 4), ("y", "core", "z", "x"))
    aux, orb = ("y", "core"), ("z", "x")
    return jax.shard_map(
        per_device,
        mesh=split,
        in_specs=(P(orb, None), P(aux, orb, None, None, None), P(orb, None)),
        out_specs=P(orb, None, aux, None),
        check_vma=False,
    )
```
